256 devices in a mesh: head: 2 (over x_lo), inner: 16 (over y, x_hi, core), outer: 8 (over z).
Axes of the slice: x: 4 (x_hi: 2, x_lo: 2; x = x_hi * 2 + x_lo), y: 4, z: 8, core: 2. Of those that a mesh axis runs over, the one named last changes fastest.
Arguments:
- query: bfloat16 [16384, 1792], P(('head', 'inner', 'outer')), may hold values from -12.5 to 12.5
- key: bfloat16 [16384, 256], P(('head', 'inner', 'outer')), may hold values from -2.5 to 2.5
- value: bfloat16 [16384, 256], P(('head', 'inner', 'outer')), may hold values from -6 to 6
- grad_out: bfloat16 [16384, 1792], P(('head', 'inner', 'outer')), may hold values from -288 to 288
Outputs:
- grad_query: bfloat16 [16384, 1792], P(('head', 'inner', 'outer'))
- grad_key: bfloat16 [16384, 256], P(('head', 'inner', 'outer'))
- grad_value: bfloat16 [16384, 256], P(('head', 'inner', 'outer'))
The draws below stay inside these ranges and needn't reach their ends.
All inputs are finite; a program needn't handle non-finite values.
Results may differ from the reference program's by a relative error of at most 0.02.
Values may be sent and summed in bfloat16 or wider, within the bound.
A program may use at most 64 MiB of HBM per device.

```python
import math
import jax
import jax.numpy as jnp
from jax import lax

ROWS = 64
HQ = 14
HK = 2
DH = 128
HALF = 4
SEQ = 8192
TOKENS = 16384


def draw_query(key, part):
    key = jax.random.fold_in(key, 1)
    base = jnp.clip(jax.random.normal(key, (TOKENS, HQ, DH), jnp.float32), -3.0, 3.0)
    return base.reshape(TOKENS, HQ * DH).astype(jnp.bfloat16)


def draw_key(key, part):
    key = jax.random.fold_in(key, 2)
    base = jnp.clip(jax.random.normal(key, (TOKENS, HK, DH), jnp.float32), -2.5, 2.5)
    return base.reshape(TOKENS, HK * DH).astype(jnp.bfloat16)


def block_levels(rng, dims, shards, smallest, largest):
    def one(dim, shards_of):
        draws = jax.random.uniform(jax.random.fold_in(jax.random.fold_in(rng, 6), dim), (shards_of,), jnp.float32, smallest / len(shards), largest / len(shards))
        return jnp.repeat(jnp.exp(draws), dims[dim] // shards_of).reshape((-1,) + (1,) * (len(dims) - dim - 1))

    factor_of = one(*shards[0])
    for cut in shards[1:]:
        factor_of = factor_of * one(*cut)
    return factor_of


def gaussian(own_key, shape, spread, most, shards=(), held_as=jnp.bfloat16):
    values = spread * jax.random.normal(own_key, shape, jnp.float32)
    if shards:
        values = values * block_levels(own_key, shape, shards, -0.22, 0.18)
    return jnp.clip(values, -most, most).astype(held_as)


def setup_inputs(seed: int = 0) -> dict:
    key_list = jax.random.split(jax.random.key(seed), 5)
    return {
        "query": draw_query(jax.random.fold_in(key_list[4], 71), 0),
        "key": draw_key(jax.random.fold_in(key_list[4], 71), 0),
        "value": gaussian(key_list[2], (TOKENS, HK * DH), 1.0, 6.0, ((0, 256),)),
        "grad_out": gaussian(key_list[3], (TOKENS, HQ * DH), 48.0, 288.0, ((0, 256),)),
    }


def block_size(total_rows):
    block_rows = min(total_rows, 512)
    while total_rows % block_rows != 0:
        block_rows = block_rows - 1
    return block_rows

def split_blocks(matrix, block_rows):
    return matrix.reshape((matrix.shape[0] // block_rows, block_rows) + matrix.shape[1:])

def to_sequences(matrix):
    width = matrix.shape[1]
    return jnp.swapaxes(matrix.reshape(-1, 2, HALF * ROWS, width), 0, 1).reshape(2, SEQ, width)

def from_sequences(matrix):
    width = matrix.shape[2]
    return jnp.swapaxes(matrix.reshape(2, -1, HALF * ROWS, width), 0, 1).reshape(TOKENS, width)

def sequence_backward(query, key, value, grad_out):
    score_scale = 1.0 / math.sqrt(DH)
    group_size = HQ // HK
    block_rows = block_size(SEQ)
    queries = query.reshape(SEQ, HQ, DH)
    out_grads = grad_out.reshape(SEQ, HQ, DH)
    keys = key.reshape(SEQ, HK, DH)
    values = value.reshape(SEQ, HK, DH)
    key_total = jnp.zeros((SEQ, HK, DH), jnp.float32)
    value_total = jnp.zeros((SEQ, HK, DH), jnp.float32)
    query_heads = []
    for head in range(HQ):
        shared = head // group_size
        key_head = keys[:, shared, :].astype(jnp.float32)
        value_head = values[:, shared, :].astype(jnp.float32)
        key_flip = key_head.T
        value_flip = value_head.T

        def fold_block(totals, blocks):
            query_block = blocks[0].astype(jnp.float32)
            grad_block = blocks[1].astype(jnp.float32)
            scores = jnp.dot(query_block, key_flip, preferred_element_type=jnp.float32) * score_scale
            top = lax.optimization_barrier(jnp.max(scores, axis=1, keepdims=True))
            log_norm = top + jnp.log(lax.optimization_barrier(jnp.sum(jnp.exp(scores - top), axis=1, keepdims=True)))
            probs = jnp.exp(scores - log_norm)
            prob_grad = jnp.dot(grad_block, value_flip, preferred_element_type=jnp.float32)
            mean_dot = lax.optimization_barrier(jnp.sum(probs * prob_grad, axis=1, keepdims=True))
            score_grad = probs * (prob_grad - mean_dot)
            probs_low = probs.astype(jnp.bfloat16).astype(jnp.float32)
            grad_low = score_grad.astype(jnp.bfloat16).astype(jnp.float32)
            key_sum, value_sum = totals
            value_sum = value_sum + jnp.dot(probs_low.T, grad_block, preferred_element_type=jnp.float32)
            key_sum = key_sum + jnp.dot(grad_low.T, query_block, preferred_element_type=jnp.float32) * score_scale
            query_grad = jnp.dot(grad_low, key_head, preferred_element_type=jnp.float32) * score_scale
            return ((key_sum, value_sum), query_grad)
        start_sums = (jnp.zeros((SEQ, DH), jnp.float32), jnp.zeros((SEQ, DH), jnp.float32))
        blocks = (split_blocks(queries[:, head, :], block_rows), split_blocks(out_grads[:, head, :], block_rows))
        (key_sum, value_sum), query_grads = lax.scan(fold_block, start_sums, blocks)
        key_total = key_total.at[:, shared, :].add(key_sum)
        value_total = value_total.at[:, shared, :].add(value_sum)
        query_heads.append(query_grads.reshape(SEQ, DH).astype(jnp.bfloat16))
    grad_query = jnp.stack(query_heads, axis=1).reshape(SEQ, HQ * DH)
    grad_key = key_total.astype(jnp.bfloat16).reshape(SEQ, HK * DH)
    grad_value = value_total.astype(jnp.bfloat16).reshape(SEQ, HK * DH)
    return (grad_query, grad_key, grad_value)

def reference(query, key, value, grad_out):
    query_seqs = to_sequences(query)
    key_seqs = to_sequences(key)
    value_seqs = to_sequences(value)
    grad_seqs = to_sequences(grad_out)
    query_parts = []
    key_parts = []
    value_parts = []
    for seq_index in range(2):
        parts = sequence_backward(query_seqs[seq_index], key_seqs[seq_index], value_seqs[seq_index], grad_seqs[seq_index])
        query_parts.append(parts[0])
        key_parts.append(parts[1])
        value_parts.append(parts[2])
    grad_query = from_sequences(jnp.stack(query_parts))
    grad_key = from_sequences(jnp.stack(key_parts))
    grad_value = from_sequences(jnp.stack(value_parts))
    return (grad_query, grad_key, grad_value)
```

```python
import functools
import math

import jax
import jax.numpy as jnp
from jax import lax
from jax.experimental import pallas as pl
from jax.experimental.pallas import tpu as pltpu
from jax.sharding import PartitionSpec as P

HQ = 14
HK = 2
DH = 128
ROWS = 64
GROUP = HQ // HK
NX = 4
NY = 4
NZ = 4
QROWS = NX * GROUP * ROWS
KEYS = NZ * 2 * ROWS
SCALE = 1.0 / math.sqrt(DH)
SCALE2 = SCALE * math.log2(math.e)
F32 = jnp.float32
BF16 = jnp.bfloat16


def dot(left, right, left_dim, right_dim):
    return lax.dot_general(
        left, right, (((left_dim,), (right_dim,)), ((), ())), preferred_element_type=F32
    )


def kernel(
    q_in, k_in, v_in, g_in, dq_out, dk_out, dv_out,
    qg_stage, kv_stage, qg_all, kv_all, m_ref, l_ref, d_ref, stat_own, stat_other,
    dq_acc, dkv, core_rx, y_sum, y_rx, z_sum, z_rx, swap_tx, swap_rx, dq_stage, dq_rx,
    swap_sem, qg_send, qg_recv, z_send, y_send, c_send, kv_recv, stat_sem,
    dc_send, dc_recv, dy_send, dy_recv, dz_send, dz_recv, ds_sem, dq_send, dq_recv,
):
    xl = lax.axis_index("head")
    inner = lax.axis_index("inner")
    outer = lax.axis_index("outer")
    y = inner // 4
    xh = (inner // 2) % 2
    c = inner % 2
    zs = outer % NZ
    z0 = outer - zs
    x = 2 * xh + xl

    def at_x(step):
        other = (x + step) % NX
        return other, {"inner": 4 * y + 2 * (other // 2) + c, "head": other % 2}

    def at_y(step):
        other = (y + step) % NY
        return other, {"inner": 4 * other + 2 * xh + c}

    def at_z(step):
        other = (zs + step) % NZ
        return other, {"outer": z0 + other}

    at_core = {"inner": 4 * y + 2 * xh + 1 - c}
    at_swap = {"head": 1 - xl}
    at_half = {"inner": 4 * y + 2 * (1 - xh) + c}

    def remote(src, dst, send_sem, recv_sem, device):
        return pltpu.make_async_remote_copy(
            src_ref=src, dst_ref=dst, send_sem=send_sem, recv_sem=recv_sem,
            device_id=device, device_id_type=pl.DeviceIdType.MESH,
        )

    barrier = pltpu.get_barrier_semaphore()
    partners = [at(step)[1] for at in (at_x, at_y, at_z) for step in (1, 2, 3)] + [at_core]
    for device in partners:
        pl.semaphore_signal(barrier, inc=1, device_id=device, device_id_type=pl.DeviceIdType.MESH)

    mine = pl.ds(pl.multiple_of(xl * DH, DH), DH)
    theirs = pl.ds(pl.multiple_of((1 - xl) * DH, DH), DH)
    kv_stage[0] = k_in[:, theirs]
    kv_stage[1] = v_in[:, theirs]
    kv_all[c, y, zs, 0, xl] = k_in[:, mine]
    kv_all[c, y, zs, 1, xl] = v_in[:, mine]
    for head in range(HQ):
        columns = pl.ds(head * DH, DH)
        qg_stage[head // GROUP, 0, head % GROUP] = q_in[:, columns]
        qg_stage[head // GROUP, 1, head % GROUP] = g_in[:, columns]
    pl.semaphore_wait(barrier, len(partners))

    swap = remote(kv_stage, kv_all.at[c, y, zs, :, xl], swap_sem.at[0], swap_sem.at[1], at_swap)
    swap.start()
    sends = []
    for step in (1, 3, 2):
        other, device = at_x(step)
        copy = remote(
            qg_stage.at[other % 2], qg_all.at[:, x], qg_send.at[step - 1], qg_recv.at[x], device
        )
        copy.start()
        sends.append(copy)
    qg_all[:, x] = qg_stage[xl]

    swap.wait()

    def chunk_copy(core, ypos, zpos, send_sem, device):
        place = kv_all.at[core, ypos, zpos]
        return remote(place, place, send_sem, kv_recv.at[core, ypos, zpos], device)

    for step in (1, 3, 2):
        copy = chunk_copy(c, y, zs, z_send.at[step - 1], at_z(step)[1])
        copy.start()
        sends.append(copy)
    for step in range(NZ):
        zpos = (zs + step) % NZ
        if step:
            chunk_copy(c, y, zpos, z_send.at[0], at_z(step)[1]).wait_recv()
        for ystep in (1, 3, 2):
            copy = chunk_copy(c, y, zpos, y_send.at[ystep - 1, step], at_y(ystep)[1])
            copy.start()
            sends.append(copy)
        copy = chunk_copy(c, y, zpos, c_send.at[0, step], at_core)
        copy.start()
        sends.append(copy)
    for ystep in (1, 3, 2):
        ypos, device = at_y(ystep)
        for step in range(NZ):
            zpos = (zs + step) % NZ
            chunk_copy(c, ypos, zpos, y_send.at[0, 0], device).wait_recv()
            copy = chunk_copy(c, ypos, zpos, c_send.at[ystep, step], at_core)
            copy.start()
            sends.append(copy)
    for step in (1, 3, 2):
        other, device = at_x(step)
        remote(
            qg_stage.at[0], qg_all.at[:, other], qg_send.at[0], qg_recv.at[other], device
        ).wait_recv()

    queries = qg_all.at[0].reshape(QROWS, DH)
    out_grads = qg_all.at[1].reshape(QROWS, DH)

    def stats_block(core, ypos):
        keys = kv_all[core, ypos, :, 0].reshape(KEYS, DH)
        values = kv_all[core, ypos, :, 1].reshape(KEYS, DH)
        scores = dot(keys, queries[...], 1, 1)
        prob_grad = dot(values, out_grads[...], 1, 1)
        old = m_ref[...]
        new = jnp.maximum(old, jnp.max(scores, axis=0, keepdims=True) * SCALE2)
        factor = jnp.exp2(old - new)
        weights = jnp.exp2(scores * SCALE2 - new)
        l_ref[...] = l_ref[...] * factor + jnp.sum(weights, axis=0, keepdims=True)
        d_ref[...] = d_ref[...] * factor + jnp.sum(weights * prob_grad, axis=0, keepdims=True)
        m_ref[...] = new

    m_ref[...] = jnp.full_like(m_ref, -1e30)
    l_ref[...] = jnp.zeros_like(l_ref)
    d_ref[...] = jnp.zeros_like(d_ref)

    def own_stats(step, carry):
        stats_block(c, (y + step) % NY)
        return carry

    lax.fori_loop(0, NY, own_stats, 0)

    for ystep in range(NY):
        for step in range(NZ):
            chunk_copy(
                1 - c, (y + ystep) % NY, (zs + step) % NZ, c_send.at[0, 0], at_core
            ).wait_recv()

    def other_stats(step, carry):
        stats_block(1 - c, (y + step) % NY)
        return carry

    lax.fori_loop(0, NY, other_stats, 0)

    stat_own[0:1] = m_ref[...]
    stat_own[1:2] = l_ref[...]
    stat_own[2:3] = d_ref[...]
    copy = remote(stat_own, stat_other, stat_sem.at[0], stat_sem.at[1], at_half)
    copy.start()
    dq_acc[...] = jnp.zeros_like(dq_acc)
    copy.wait()
    top = jnp.maximum(stat_own[0:1], stat_other[0:1])
    own_factor = jnp.exp2(stat_own[0:1] - top)
    other_factor = jnp.exp2(stat_other[0:1] - top)
    total = stat_own[1:2] * own_factor + stat_other[1:2] * other_factor
    m_ref[...] = top + jnp.log2(total)
    d_ref[...] = (stat_own[2:3] * own_factor + stat_other[2:3] * other_factor) / total

    def grad_block(core, ypos):
        keys = kv_all[core, ypos, :, 0].reshape(KEYS, DH)
        values = kv_all[core, ypos, :, 1].reshape(KEYS, DH)
        scores = dot(keys, queries[...], 1, 1)
        prob_grad = dot(values, out_grads[...], 1, 1)
        probs = jnp.exp2(scores * SCALE2 - m_ref[...])
        grad_low = (probs * (prob_grad - d_ref[...])).astype(BF16)
        value_term = dot(probs.astype(BF16), out_grads[...], 1, 0)
        key_term = dot(grad_low, queries[...], 1, 0) * SCALE
        dq_acc[...] += dot(keys, grad_low, 0, 0)
        return key_term, value_term

    def core_copy(ypos):
        return remote(
            dkv.at[ypos], core_rx.at[ypos], dc_send.at[ypos], dc_recv.at[ypos], at_core
        )

    def other_grads(step, carry):
        ypos = (y + 1 + step) % NY
        key_term, value_term = grad_block(1 - c, ypos)
        dkv[ypos, :, 0] = key_term.astype(BF16).reshape(NZ, 2, ROWS, DH)
        dkv[ypos, :, 1] = value_term.astype(BF16).reshape(NZ, 2, ROWS, DH)
        core_copy(ypos).start()
        return carry

    lax.fori_loop(0, NY, other_grads, 0)

    def y_copy(slot, sender, device, sem):
        return remote(y_sum.at[slot], y_rx.at[sender], sem, dy_recv.at[sender], device)

    def own_grads(step, carry):
        ypos, device = at_y(1 + step)
        key_term, value_term = grad_block(c, ypos)
        core_copy(ypos).wait_recv()
        shape = (NZ, 2, ROWS, DH)
        y_sum[ypos, :, 0] = (key_term.reshape(shape) + core_rx[ypos, :, 0].astype(F32)).astype(BF16)
        y_sum[ypos, :, 1] = (value_term.reshape(shape) + core_rx[ypos, :, 1].astype(F32)).astype(BF16)

        @pl.when(step < NY - 1)
        def send():
            y_copy(ypos, y, device, dy_send.at[step]).start()

        return carry

    lax.fori_loop(0, NY, own_grads, 0)

    dq_rows = (dq_acc[...] * SCALE).T.astype(BF16)
    dq_stage[...] = dq_rows.reshape(NX, GROUP, ROWS, DH)
    for step in (2, 1, 3):
        other, device = at_x(step)
        copy = remote(
            dq_stage.at[other], dq_rx.at[x], dq_send.at[step - 1], dq_recv.at[x], device
        )
        copy.start()
        sends.append(copy)
    dq_rx[x] = dq_stage[x]

    for step in (1, 2, 3):
        ypos, device = at_y(step)
        y_copy(ypos, ypos, device, dy_send.at[0]).wait_recv()
    total = y_sum[y].astype(F32)
    for step in (1, 2, 3):
        total = total + y_rx[(y + step) % NY].astype(F32)
    z_sum[...] = total.astype(BF16)
    for step in (1, 2, 3):
        other, device = at_z(step)
        copy = remote(
            z_sum.at[other], z_rx.at[zs], dz_send.at[step - 1], dz_recv.at[zs], device
        )
        copy.start()
        sends.append(copy)
    for step in (1, 2, 3):
        other, device = at_z(step)
        remote(
            z_sum.at[other], z_rx.at[other], dz_send.at[0], dz_recv.at[other], device
        ).wait_recv()
    total = z_sum[zs].astype(F32)
    for step in (1, 2, 3):
        total = total + z_rx[(zs + step) % NZ].astype(F32)
    swap_tx[...] = total.astype(BF16)
    copy = remote(swap_tx.at[:, 1 - xl], swap_rx, ds_sem.at[0], ds_sem.at[1], at_swap)
    copy.start()
    dk_out[:, mine] = swap_tx[0, xl]
    dv_out[:, mine] = swap_tx[1, xl]

    for step in (1, 3, 2):
        other, device = at_x(step)
        remote(
            dq_stage.at[other], dq_rx.at[other], dq_send.at[0], dq_recv.at[other], device
        ).wait_recv()
    for head in range(HQ):
        group, place = head // GROUP, head % GROUP
        both = dq_rx[group, place].astype(F32) + dq_rx[group + 2, place].astype(F32)
        dq_out[:, pl.ds(head * DH, DH)] = both.astype(BF16)

    copy.wait()
    dk_out[:, theirs] = swap_rx[0]
    dv_out[:, theirs] = swap_rx[1]

    for copy in sends:
        copy.wait_send()
    for ypos in range(NY):
        core_copy(ypos).wait_send()
    for step in range(NY - 1):
        ypos, device = at_y(1 + step)
        y_copy(ypos, y, device, dy_send.at[step]).wait_send()


def on_device(query, key, value, grad_out):
    vmem = pl.BlockSpec(memory_space=pltpu.VMEM)
    dma = pltpu.SemaphoreType.DMA
    return pl.pallas_call(
        kernel,
        out_shape=(
            jax.ShapeDtypeStruct(query.shape, BF16),
            jax.ShapeDtypeStruct(key.shape, BF16),
            jax.ShapeDtypeStruct(value.shape, BF16),
        ),
        in_specs=[vmem] * 4,
        out_specs=(vmem,) * 3,
        scratch_shapes=[
            pltpu.VMEM((HK, 2, GROUP, ROWS, DH), BF16),
            pltpu.VMEM((2, ROWS, DH), BF16),
            pltpu.VMEM((2, NX, GROUP, ROWS, DH), BF16),
            pltpu.VMEM((2, NY, NZ, 2, 2, ROWS, DH), BF16),
            pltpu.VMEM((1, QROWS), F32),
            pltpu.VMEM((1, QROWS), F32),
            pltpu.VMEM((1, QROWS), F32),
            pltpu.VMEM((8, QROWS), F32),
            pltpu.VMEM((8, QROWS), F32),
            pltpu.VMEM((DH, QROWS), F32),
            pltpu.VMEM((NY, NZ, 2, 2, ROWS, DH), BF16),
            pltpu.VMEM((NY, NZ, 2, 2, ROWS, DH), BF16),
            pltpu.VMEM((NY, NZ, 2, 2, ROWS, DH), BF16),
            pltpu.VMEM((NY, NZ, 2, 2, ROWS, DH), BF16),
            pltpu.VMEM((NZ, 2, 2, ROWS, DH), BF16),
            pltpu.VMEM((NZ, 2, 2, ROWS, DH), BF16),
            pltpu.VMEM((2, 2, ROWS, DH), BF16),
            pltpu.VMEM((2, ROWS, DH), BF16),
            pltpu.VMEM((NX, GROUP, ROWS, DH), BF16),
            pltpu.VMEM((NX, GROUP, ROWS, DH), BF16),
            dma((2,)),
            dma((3,)),
            dma((NX,)),
            dma((3,)),
            dma((3, NZ)),
            dma((NY, NZ)),
            dma((2, NY, NZ)),
            dma((2,)),
            dma((NY,)),
            dma((NY,)),
            dma((3,)),
            dma((NY,)),
            dma((3,)),
            dma((NZ,)),
            dma((2,)),
            dma((3,)),
            dma((NX,)),
        ],
        compiler_params=pltpu.CompilerParams(
            collective_id=0, has_side_effects=True, vmem_limit_bytes=60 * 2**20
        ),
    )(query, key, value, grad_out)


def solution(mesh):
    spec = P(("head", "inner", "outer"), None)
    return jax.shard_map(
        on_device, mesh=mesh, in_specs=(spec,) * 4, out_specs=(spec,) * 3, check_vma=False
    )
```

```python
import functools
import math

import jax
import jax.numpy as jnp
from jax import lax
from jax.experimental import pallas as pl
from jax.experimental.pallas import tpu as pltpu
from jax.sharding import PartitionSpec as P

HQ = 14
HK = 2
DH = 128
ROWS = 64
GROUP = HQ // HK
NX = 4
NY = 4
NZ = 4
QROWS = NX * GROUP * ROWS
BLOCK = NZ * 2 * ROWS
HALF = 2 * 2 * ROWS
SCALE = 1.0 / math.sqrt(DH)
SCALE2 = SCALE * math.log2(math.e)
F32 = jnp.float32
BF16 = jnp.bfloat16


def dot(left, right, left_dim, right_dim):
    return lax.dot_general(
        left, right, (((left_dim,), (right_dim,)), ((), ())), preferred_element_type=F32
    )


def kernel(
    q_in, k_in, v_in, g_in, dq_out, dk_out, dv_out,
    q_buf, k_buf, v_buf, g_buf,
    qg_stage, kv_stage, qg_all, kv_all, e_ref, mb_ref, stat_own, stat_other, lse_ref, mean_ref,
    dq_acc, dkv, core_rx, y_sum, y_rx, z_sum, z_rx, dq_stage, dq_rx,
    in_sem, qg_send, qg_recv, z_send, piece_recv, y_send, f_send, chunk_recv, c_send, c_recv,
    stat_sem, dc_send, dc_recv, dy_send, dy_recv, dz_send, dz_recv,
    dq_send, dq_recv,
):
    xl = lax.axis_index("head")
    inner = lax.axis_index("inner")
    outer = lax.axis_index("outer")
    y = inner // 4
    xh = (inner // 2) % 2
    c = inner % 2
    zs = outer % NZ
    z0 = outer - zs
    zq = zs // 2

    def at_x(pair, other):
        return {"inner": 4 * y + 2 * other + c, "head": (xl + 1 - pair) % 2}

    def at_y(step):
        other = (y + step) % NY
        return other, {"inner": 4 * other + 2 * xh + c}

    def at_z(step):
        other = (zs + step) % NZ
        return other, {"outer": z0 + other}

    at_core = {"inner": 4 * y + 2 * xh + 1 - c}
    at_swap = {"head": 1 - xl}
    at_half = {"inner": 4 * y + 2 * (1 - xh) + c}

    def remote(src, dst, send_sem, recv_sem, device):
        return pltpu.make_async_remote_copy(
            src_ref=src, dst_ref=dst, send_sem=send_sem, recv_sem=recv_sem,
            device_id=device, device_id_type=pl.DeviceIdType.MESH,
        )

    barrier = pltpu.get_barrier_semaphore()
    x_partners = [(0, xh), (0, 1 - xh), (1, 1 - xh)]
    partners = [at_x(*place) for place in x_partners]
    partners += [at(step)[1] for at in (at_y, at_z) for step in (1, 2, 3)] + [at_core]
    partners += [{**at_z(step)[1], **at_swap} for step in (1, 2, 3)]
    for device in partners:
        pl.semaphore_signal(barrier, inc=1, device_id=device, device_id_type=pl.DeviceIdType.MESH)

    loads = [
        pltpu.make_async_copy(src, dst, in_sem.at[place])
        for place, (src, dst) in enumerate(
            [(k_in, k_buf), (v_in, v_buf), (q_in, q_buf), (g_in, g_buf)]
        )
    ]
    for load in loads:
        load.start()
    mine = pl.ds(pl.multiple_of(xl * DH, DH), DH)
    theirs = pl.ds(pl.multiple_of((1 - xl) * DH, DH), DH)
    for load in loads:
        load.wait()
    kv_stage[0] = k_buf[:, theirs]
    kv_stage[1] = v_buf[:, theirs]
    kv_all[y, c, zs, xl, 0] = k_buf[:, mine]
    kv_all[y, c, zs, xl, 1] = v_buf[:, mine]
    for head in range(HQ):
        columns = pl.ds(head * DH, DH)
        qg_stage[head // GROUP, 0, head % GROUP] = q_buf[:, columns]
        qg_stage[head // GROUP, 1, head % GROUP] = g_buf[:, columns]
    qg_all[:, 1, xh] = qg_stage[xl]
    pl.semaphore_wait(barrier, len(partners))

    sends = []

    def begin(copy):
        copy.start()
        sends.append(copy)

    def piece_copy(src, zpos, part, send_sem, device):
        return remote(src, kv_all.at[y, c, zpos, part], send_sem, piece_recv.at[zpos, part], device)

    swap = piece_copy(kv_stage, zs, xl, z_send.at[0, 0], at_swap)
    swap.start()
    for step in (1, 3, 2):
        begin(piece_copy(kv_all.at[y, c, zs, xl], zs, xl, z_send.at[step, 0], at_z(step)[1]))

    def query_copy(place):
        pair, other = x_partners[place]
        return remote(
            qg_stage.at[(xl + 1 - pair) % 2], qg_all.at[:, pair, xh], qg_send.at[place],
            qg_recv.at[pair, xh], at_x(pair, other),
        )

    def wait_queries(place):
        pair, other = x_partners[place]
        remote(
            qg_stage.at[0], qg_all.at[:, pair, other], qg_send.at[place], qg_recv.at[pair, other],
            at_x(pair, other),
        ).wait_recv()

    begin(query_copy(0))
    begin(query_copy(1))

    def chunk_copy(ypos, zpos, send_sem, device):
        place = kv_all.at[ypos, c, zpos]
        return remote(place, place, send_sem, chunk_recv.at[ypos, zpos], device)

    def block_copy(ypos, core):
        place = kv_all.at[ypos, core]
        return remote(place, place, c_send.at[ypos], c_recv.at[ypos, core], at_core)

    def forward_copy(step):
        ystep, target = (1, 3) if step < 2 else (3, 1)
        return chunk_copy(
            (y + ystep) % NY, (zs + step) % NZ, f_send.at[step], at_y(target)[1]
        )

    piece_copy(kv_stage, zs, 1 - xl, z_send.at[0, 0], at_swap).wait_recv()
    for step in (1, 3, 2):
        place = kv_all.at[y, c, zs, 1 - xl]
        begin(piece_copy(place, zs, 1 - xl, z_send.at[step, 1], at_z(step)[1]))
    for step in (0, 1, 3, 2):
        zpos, device = at_z(step)
        if step:
            for part in (xl, 1 - xl):
                piece_copy(kv_stage, zpos, part, z_send.at[0, 0], device).wait_recv()
        for place, ystep in enumerate((1, 3)):
            begin(chunk_copy(y, zpos, y_send.at[place, step], at_y(ystep)[1]))
        if step == 0:
            begin(query_copy(2))
    begin(block_copy(y, c))

    def wait_chunk(ystep, step):
        ypos, device = at_y(ystep)
        chunk_copy(ypos, (zs + step) % NZ, y_send.at[0, 0], device).wait_recv()

    for step in (0, 1, 3, 2):
        for ystep in (1, 3):
            wait_chunk(ystep, step)
            if (step < 2) == (ystep == 1):
                begin(forward_copy(step))
    for ystep in (1, 3):
        begin(block_copy((y + ystep) % NY, c))
    for place in range(3):
        wait_queries(place)

    queries = qg_all.at[0].reshape(QROWS, DH)
    out_grads = qg_all.at[1].reshape(QROWS, DH)

    def stat_copy():
        return remote(stat_own, stat_other, stat_sem.at[0], stat_sem.at[1], at_half)

    def wait_core(ystep):
        block_copy((y + ystep) % NY, 1 - c).wait_recv()

    stat_own[...] = jnp.zeros_like(stat_own)
    stat_own[0:1] = jnp.full((1, QROWS), -1e30, F32)

    def stats_step(turn, carry):
        @pl.when(turn == 1)
        def first():
            wait_core(0)

        @pl.when(turn == 3)
        def second():
            wait_core(1)

        @pl.when(turn == 4)
        def opposite():
            for step in range(NZ):
                wait_chunk(2, step)
            block_copy((y + 2) % NY, c).start()

        @pl.when(turn == 5)
        def third():
            wait_core(3)

        @pl.when(turn == 7)
        def last():
            wait_core(2)

        slot, role = turn // 2, turn % 2
        ypos = (y + slot + slot // 2 - 2 * (slot // 3)) % NY
        core = c + role * (1 - 2 * c)
        keys = kv_all[ypos, core, :, :, 0].reshape(BLOCK, DH)
        values = kv_all[ypos, core, :, :, 1].reshape(BLOCK, DH)
        scores = dot(keys, queries[...], 1, 1)
        prob_grad = dot(values, out_grads[...], 1, 1)
        old = stat_own[0:1]
        new = jnp.maximum(old, jnp.max(scores, axis=0, keepdims=True) * SCALE2)
        factor = jnp.exp2(old - new)
        weights = jnp.exp2(scores * SCALE2 - new)
        e_ref[ypos, core] = weights.astype(BF16)
        mb_ref[ypos, core] = new
        stat_own[0:1] = new
        stat_own[1:2] = stat_own[1:2] * factor + jnp.sum(weights, axis=0, keepdims=True)
        stat_own[2:3] = stat_own[2:3] * factor + jnp.sum(
            weights * prob_grad, axis=0, keepdims=True
        )
        return carry

    lax.fori_loop(0, 2 * NY, stats_step, 0)

    copy = stat_copy()
    copy.start()
    dq_acc[...] = jnp.zeros_like(dq_acc)
    copy.wait()
    top = jnp.maximum(stat_own[0:1], stat_other[0:1])
    own_factor = jnp.exp2(stat_own[0:1] - top)
    other_factor = jnp.exp2(stat_other[0:1] - top)
    total = stat_own[1:2] * own_factor + stat_other[1:2] * other_factor
    weighted = stat_own[2:3] * own_factor + stat_other[2:3] * other_factor
    lse_ref[...] = top + jnp.log2(total)
    mean_ref[...] = weighted / total

    def grad_block(ypos, core, half):
        keys = kv_all[ypos, core, pl.ds(2 * half, 2), :, 0].reshape(HALF, DH)
        values = kv_all[ypos, core, pl.ds(2 * half, 2), :, 1].reshape(HALF, DH)
        prob_grad = dot(values, out_grads[...], 1, 1)
        factor = jnp.exp2(mb_ref[ypos, core] - lse_ref[...])
        place = pl.ds(pl.multiple_of(half * HALF, HALF), HALF)
        probs = e_ref[ypos, core, place, :].astype(F32) * factor
        grad_low = (probs * (prob_grad - mean_ref[...])).astype(BF16)
        value_term = dot(probs.astype(BF16), out_grads[...], 1, 0)
        key_term = dot(grad_low, queries[...], 1, 0) * SCALE
        dq_acc[...] += dot(keys, grad_low, 0, 0)
        return key_term, value_term

    def core_copy(ypos, half):
        place = pl.ds(2 * half, 2)
        return remote(
            dkv.at[ypos, place], core_rx.at[ypos, place], dc_send.at[ypos, half],
            dc_recv.at[ypos, half], at_core,
        )

    def y_copy(ypos, sender, half, device):
        place = pl.ds(2 * half, 2)
        return remote(
            y_sum.at[ypos, place], y_rx.at[sender, place], dy_send.at[ypos, half],
            dy_recv.at[sender, half], device,
        )

    def y_total(half):
        place = pl.ds(2 * half, 2)
        for step in (1, 2, 3):
            ypos, device = at_y(step)
            y_copy(ypos, ypos, half, device).wait_recv()
        total = y_sum[y, place].astype(F32)
        for step in (1, 2, 3):
            total = total + y_rx[(y + step) % NY, place].astype(F32)
        z_sum[place] = total.astype(BF16)

    def z_copy(zpos, part, place):
        return remote(
            z_sum.at[zpos, part], z_rx.at[zs, xl], dz_send.at[place], dz_recv.at[zs, xl],
            {"outer": z0 + zpos, "head": part},
        )

    def wait_z(zpos, part):
        remote(
            z_sum.at[zpos, part], z_rx.at[zpos, part], dz_send.at[0], dz_recv.at[zpos, part],
            {"outer": z0 + zpos, "head": part},
        ).wait_recv()

    far_places = [(2 * (1 - zq) + place // 2, place % 2, place) for place in range(4)]
    near = 4 * zq + 1 - zs
    near_places = [(near, 0, 4), (near, 1, 5), (zs, 1 - xl, 6)]

    def grad_place(turn):
        late, slot = turn % 2, turn // 2
        half = (1 - late) * (1 - zq) + late * zq
        ystep = ((1 - slot // 2) * (2 - slot) + slot // 2 * (slot + 1)) % NY
        return half, slot, at_y(ystep)

    def put_other(ypos, half, terms):
        place = pl.ds(2 * half, 2)
        for kind, term in enumerate(terms):
            dkv[ypos, place, :, kind] = term.astype(BF16).reshape(2, 2, ROWS, DH)
        core_copy(ypos, half).start()

    def put_own(ypos, half, terms):
        place = pl.ds(2 * half, 2)
        core_copy(ypos, half).wait_recv()
        for kind, term in enumerate(terms):
            total = term.reshape(2, 2, ROWS, DH) + core_rx[ypos, place, :, kind].astype(F32)
            y_sum[ypos, place, :, kind] = total.astype(BF16)

    def grad_step(index, carry):
        own = 1 - index % 2 - (1 - (index + 14) // 15) + index // 15
        half, slot, (ypos, device) = grad_place((index + 1) // 2 - own)

        @pl.when(index == 15)
        def far_sums():
            y_total(1 - zq)
            for far in far_places:
                z_copy(*far).start()

        terms = grad_block(ypos, 1 - c + own * (2 * c - 1), half)

        @pl.when(own == 0)
        def pass_on():
            put_other(ypos, half, terms)

        @pl.when(own == 1)
        def keep():
            put_own(ypos, half, terms)

            @pl.when(slot < NY - 1)
            def send():
                y_copy(ypos, y, half, device).start()

        return carry

    lax.fori_loop(0, 4 * NY, grad_step, 0)

    dq_rows = (dq_acc[...] * SCALE).T.astype(BF16)
    dq_stage[...] = dq_rows.reshape(2, 2, GROUP, ROWS, DH)
    for place, (pair, other) in enumerate(x_partners):
        begin(
            remote(
                dq_stage.at[pair, other], dq_rx.at[pair, xh], dq_send.at[place],
                dq_recv.at[pair, xh], at_x(pair, other),
            )
        )
    dq_rx[1, xh] = dq_stage[1, xh]
    y_total(zq)
    for near_place in near_places:
        z_copy(*near_place).start()
    z_rx[zs, xl] = z_sum[zs, xl]
    for step in (2, 3, 1):
        for part in range(2):
            wait_z(at_z(step)[0], part)
    wait_z(zs, 1 - xl)
    for head in range(HK):
        total = z_rx[0, head].astype(F32)
        for zpos in range(1, NZ):
            total = total + z_rx[zpos, head].astype(F32)
        dk_out[:, pl.ds(head * DH, DH)] = total[0].astype(BF16)
        dv_out[:, pl.ds(head * DH, DH)] = total[1].astype(BF16)

    for pair, other in x_partners:
        remote(
            dq_stage.at[0, 0], dq_rx.at[pair, other], dq_send.at[0], dq_recv.at[pair, other],
            at_x(pair, other),
        ).wait_recv()
    for head in range(HQ):
        group, place = head // GROUP, head % GROUP
        pair = (xl + group + 1) % 2
        both = dq_rx[pair, 0, place].astype(F32) + dq_rx[pair, 1, place].astype(F32)
        dq_out[:, pl.ds(head * DH, DH)] = both.astype(BF16)

    for copy in sends:
        copy.wait_send()
    swap.wait_send()
    block_copy((y + 2) % NY, c).wait_send()
    for place in far_places + near_places:
        z_copy(*place).wait_send()
    for half in range(2):
        for ypos in range(NY):
            core_copy(ypos, half).wait_send()
        for step in (1, 2, 3):
            ypos, device = at_y(step)
            y_copy(ypos, y, half, device).wait_send()


def on_device(query, key, value, grad_out):
    vmem = pl.BlockSpec(memory_space=pltpu.VMEM)
    dma = pltpu.SemaphoreType.DMA
    rows = query.shape[0]
    return pl.pallas_call(
        kernel,
        out_shape=(
            pltpu.VMEM(query.shape, BF16),
            pltpu.VMEM(key.shape, BF16),
            pltpu.VMEM(value.shape, BF16),
        ),
        in_specs=[pl.BlockSpec(memory_space=pl.ANY)] * 4,
        out_specs=(vmem,) * 3,
        scratch_shapes=[
            pltpu.VMEM((rows, HQ * DH), BF16),
            pltpu.VMEM((rows, HK * DH), BF16),
            pltpu.VMEM((rows, HK * DH), BF16),
            pltpu.VMEM((rows, HQ * DH), BF16),
            pltpu.VMEM((HK, 2, GROUP, ROWS, DH), BF16),
            pltpu.VMEM((2, ROWS, DH), BF16),
            pltpu.VMEM((2, 2, 2, GROUP, ROWS, DH), BF16),
            pltpu.VMEM((NY, 2, NZ, 2, 2, ROWS, DH), BF16),
            pltpu.VMEM((NY, 2, BLOCK, QROWS), BF16),
            pltpu.VMEM((NY, 2, 1, QROWS), F32),
            pltpu.VMEM((8, QROWS), F32),
            pltpu.VMEM((8, QROWS), F32),
            pltpu.VMEM((1, QROWS), F32),
            pltpu.VMEM((1, QROWS), F32),
            pltpu.VMEM((DH, QROWS), F32),
            pltpu.VMEM((NY, NZ, 2, 2, ROWS, DH), BF16),
            pltpu.VMEM((NY, NZ, 2, 2, ROWS, DH), BF16),
            pltpu.VMEM((NY, NZ, 2, 2, ROWS, DH), BF16),
            pltpu.VMEM((NY, NZ, 2, 2, ROWS, DH), BF16),
            pltpu.VMEM((NZ, 2, 2, ROWS, DH), BF16),
            pltpu.VMEM((NZ, 2, 2, ROWS, DH), BF16),
            pltpu.VMEM((2, 2, GROUP, ROWS, DH), BF16),
            pltpu.VMEM((2, 2, GROUP, ROWS, DH), BF16),
            dma((4,)),
            dma((3,)),
            dma((2, 2)),
            dma((NZ, 2)),
            dma((NZ, 2)),
            dma((2, NZ)),
            dma((NZ,)),
            dma((NY, NZ)),
            dma((NY,)),
            dma((NY, 2)),
            dma((2,)),
            dma((NY, 2)),
            dma((NY, 2)),
            dma((NY, 2)),
            dma((NY, 2)),
            dma((7,)),
            dma((NZ, 2)),
            dma((3,)),
            dma((2, 2)),
        ],
        compiler_params=pltpu.CompilerParams(
            collective_id=0, has_side_effects=True, vmem_limit_bytes=60 * 2**20
        ),
    )(query, key, value, grad_out)

def solution(mesh):
    spec = P(("head", "inner", "outer"), None)
    return jax.shard_map(
        on_device, mesh=mesh, in_specs=(spec,) * 4, out_specs=(spec,) * 3, check_vma=False
    )
```

```python
import functools
import math

import jax
import jax.numpy as jnp
from jax import lax
from jax.experimental import pallas as pl
from jax.experimental.pallas import tpu as pltpu
from jax.sharding import PartitionSpec as P

HQ = 14
HK = 2
DH = 128
ROWS = 64
GROUP = HQ // HK
NX = 4
NY = 4
NZ = 4
PAIR = 2 * GROUP * ROWS
QROWS = 2 * PAIR
BLOCK = NZ * 2 * ROWS
HALF = 2 * 2 * ROWS
SCALE = 1.0 / math.sqrt(DH)
SCALE2 = SCALE * math.log2(math.e)
F32 = jnp.float32
BF16 = jnp.bfloat16


def dot(left, right, left_dim, right_dim):
    return lax.dot_general(
        left, right, (((left_dim,), (right_dim,)), ((), ())), preferred_element_type=F32
    )


def kernel(
    q_in, k_in, v_in, g_in, dq_out, dk_out, dv_out,
    q_buf, k_buf, v_buf, g_buf,
    qg_stage, kv_stage, qg_all, kv_all, e_ref, mb_ref, m_ref, l_ref, d_ref, m_other, l_other, d_other, lse_ref, mean_ref,
    dq_acc, dkv, core_rx, y_sum, y_rx, z_sum, z_rx, dq_stage, dq_rx,
    in_sem, qg_send, qg_recv, z_send, piece_recv, y_send, f_send, chunk_recv, c_send, c_recv,
    stat_send, stat_recv, dc_send, dc_recv, dy_send, dy_recv, dz_send, dz_recv,
    dq_send, dq_recv,
):
    xl = lax.axis_index("head")
    inner = lax.axis_index("inner")
    outer = lax.axis_index("outer")
    y = inner // 4
    xh = (inner // 2) % 2
    c = inner % 2
    zs = outer % NZ
    z0 = outer - zs
    zq = zs // 2

    def at_x(pair, other):
        return {"inner": 4 * y + 2 * other + c, "head": (xl + 1 - pair) % 2}

    def at_y(step):
        other = (y + step) % NY
        return other, {"inner": 4 * other + 2 * xh + c}

    def at_z(step):
        other = (zs + step) % NZ
        return other, {"outer": z0 + other}

    at_core = {"inner": 4 * y + 2 * xh + 1 - c}
    at_swap = {"head": 1 - xl}
    at_half = {"inner": 4 * y + 2 * (1 - xh) + c}

    def remote(src, dst, send_sem, recv_sem, device):
        return pltpu.make_async_remote_copy(
            src_ref=src, dst_ref=dst, send_sem=send_sem, recv_sem=recv_sem,
            device_id=device, device_id_type=pl.DeviceIdType.MESH,
        )

    barrier = pltpu.get_barrier_semaphore()
    x_partners = [(0, xh), (0, 1 - xh), (1, 1 - xh)]
    partners = [at_x(*place) for place in x_partners]
    partners += [at(step)[1] for at in (at_y, at_z) for step in (1, 2, 3)] + [at_core]
    partners += [{**at_z(step)[1], **at_swap} for step in (1, 2, 3)]
    for device in partners:
        pl.semaphore_signal(barrier, inc=1, device_id=device, device_id_type=pl.DeviceIdType.MESH)

    loads = [
        pltpu.make_async_copy(src, dst, in_sem.at[place])
        for place, (src, dst) in enumerate(
            [(k_in, k_buf), (v_in, v_buf), (q_in, q_buf), (g_in, g_buf)]
        )
    ]
    for load in loads:
        load.start()
    mine = pl.ds(pl.multiple_of(xl * DH, DH), DH)
    theirs = pl.ds(pl.multiple_of((1 - xl) * DH, DH), DH)
    loads[0].wait()
    kv_stage[0] = k_buf[:, theirs]
    kv_all[y, c, zs, xl, 0] = k_buf[:, mine]
    loads[1].wait()
    kv_stage[1] = v_buf[:, theirs]
    kv_all[y, c, zs, xl, 1] = v_buf[:, mine]
    pl.semaphore_wait(barrier, len(partners))

    sends = []

    def begin(copy):
        copy.start()
        sends.append(copy)

    def piece_copy(src, zpos, part, send_sem, device):
        return remote(src, kv_all.at[y, c, zpos, part], send_sem, piece_recv.at[zpos, part], device)

    swap = piece_copy(kv_stage, zs, xl, z_send.at[0, 0], at_swap)
    swap.start()
    for step in (1, 3, 2):
        begin(piece_copy(kv_all.at[y, c, zs, xl], zs, xl, z_send.at[step, 0], at_z(step)[1]))

    def query_copy(place):
        pair, other = x_partners[place]
        return remote(
            qg_stage.at[(xl + 1 - pair) % 2], qg_all.at[:, pair, xh], qg_send.at[place],
            qg_recv.at[pair, xh], at_x(pair, other),
        )

    def wait_queries(place):
        pair, other = x_partners[place]
        remote(
            qg_stage.at[0], qg_all.at[:, pair, other], qg_send.at[place], qg_recv.at[pair, other],
            at_x(pair, other),
        ).wait_recv()

    loads[2].wait()
    loads[3].wait()
    for head in range(HQ):
        columns = pl.ds(head * DH, DH)
        qg_stage[head // GROUP, 0, head % GROUP] = q_buf[:, columns]
        qg_stage[head // GROUP, 1, head % GROUP] = g_buf[:, columns]
    begin(query_copy(0))
    begin(query_copy(1))
    qg_all[:, 1, xh] = qg_stage[xl]

    def chunk_copy(ypos, zpos, send_sem, device):
        place = kv_all.at[ypos, c, zpos]
        return remote(place, place, send_sem, chunk_recv.at[ypos, zpos], device)

    def block_copy(ypos, core):
        place = kv_all.at[ypos, core]
        return remote(place, place, c_send.at[ypos], c_recv.at[ypos, core], at_core)

    def forward_copy(step):
        ystep, target = (1, 3) if step < 2 else (3, 1)
        return chunk_copy(
            (y + ystep) % NY, (zs + step) % NZ, f_send.at[step], at_y(target)[1]
        )

    piece_copy(kv_stage, zs, 1 - xl, z_send.at[0, 0], at_swap).wait_recv()
    for step in (1, 3, 2):
        place = kv_all.at[y, c, zs, 1 - xl]
        begin(piece_copy(place, zs, 1 - xl, z_send.at[step, 1], at_z(step)[1]))
    for step in (0, 1, 3, 2):
        zpos, device = at_z(step)
        if step:
            for part in (xl, 1 - xl):
                piece_copy(kv_stage, zpos, part, z_send.at[0, 0], device).wait_recv()
        for place, ystep in enumerate((1, 3)):
            begin(chunk_copy(y, zpos, y_send.at[place, step], at_y(ystep)[1]))
        if step == 0:
            begin(query_copy(2))
    begin(block_copy(y, c))

    def wait_chunk(ystep, step):
        ypos, device = at_y(ystep)
        chunk_copy(ypos, (zs + step) % NZ, y_send.at[0, 0], device).wait_recv()

    for step in (0, 1, 3, 2):
        for ystep in (1, 3):
            wait_chunk(ystep, step)
            if (step < 2) == (ystep == 1):
                begin(forward_copy(step))
    for ystep in (1, 3):
        begin(block_copy((y + ystep) % NY, c))
    for place in range(3):
        wait_queries(place)

    queries = qg_all.at[0].reshape(QROWS, DH)
    out_grads = qg_all.at[1].reshape(QROWS, DH)

    stats = [(m_ref, m_other), (l_ref, l_other), (d_ref, d_other)]

    def stat_copy(kind):
        own, other = stats[kind]
        return remote(own, other, stat_send.at[kind], stat_recv.at[kind], at_half)

    def wait_core(ystep):
        block_copy((y + ystep) % NY, 1 - c).wait_recv()

    m_ref[...] = jnp.full_like(m_ref, -1e30)
    l_ref[...] = jnp.zeros_like(l_ref)
    d_ref[...] = jnp.zeros_like(d_ref)

    def stats_step(turn, carry):
        @pl.when(turn == 1)
        def first():
            wait_core(0)

        @pl.when(turn == 3)
        def second():
            wait_core(1)

        @pl.when(turn == 4)
        def opposite():
            for step in range(NZ):
                wait_chunk(2, step)
            block_copy((y + 2) % NY, c).start()

        @pl.when(turn == 5)
        def third():
            wait_core(3)

        @pl.when(turn == 7)
        def last():
            wait_core(2)

        slot, role = turn // 2, turn % 2
        ypos = (y + slot + slot // 2 - 2 * (slot // 3)) % NY
        core = c + role * (1 - 2 * c)
        keys = kv_all[ypos, core, :, :, 0].reshape(BLOCK, DH)
        values = kv_all[ypos, core, :, :, 1].reshape(BLOCK, DH)
        scores = dot(keys, queries[...], 1, 1)
        prob_grad = dot(values, out_grads[...], 1, 1)
        old = m_ref[...]
        new = jnp.maximum(old, jnp.max(scores, axis=0, keepdims=True) * SCALE2)
        factor = jnp.exp2(old - new)
        weights = jnp.exp2(scores * SCALE2 - new)
        e_ref[ypos, core] = weights.astype(BF16)
        mb_ref[ypos, core] = new
        m_ref[...] = new
        l_ref[...] = l_ref[...] * factor + jnp.sum(weights, axis=0, keepdims=True)
        d_ref[...] = d_ref[...] * factor + jnp.sum(weights * prob_grad, axis=0, keepdims=True)
        return carry

    lax.fori_loop(0, 2 * NY, stats_step, 0)

    for kind in range(3):
        stat_copy(kind).start()
    dq_acc[...] = jnp.zeros_like(dq_acc)
    for kind in range(3):
        stat_copy(kind).wait_recv()
    top = jnp.maximum(m_ref[...], m_other[...])
    own_factor = jnp.exp2(m_ref[...] - top)
    other_factor = jnp.exp2(m_other[...] - top)
    total = l_ref[...] * own_factor + l_other[...] * other_factor
    weighted = d_ref[...] * own_factor + d_other[...] * other_factor
    lse_ref[...] = top + jnp.log2(total)
    mean_ref[...] = weighted / total

    def grad_block(ypos, core, half):
        keys = kv_all[ypos, core, pl.ds(2 * half, 2), :, 0].reshape(HALF, DH)
        values = kv_all[ypos, core, pl.ds(2 * half, 2), :, 1].reshape(HALF, DH)
        prob_grad = dot(values, out_grads[...], 1, 1)
        factor = jnp.exp2(mb_ref[ypos, core] - lse_ref[...])
        place = pl.ds(pl.multiple_of(half * HALF, HALF), HALF)
        probs = e_ref[ypos, core, place, :].astype(F32) * factor
        grad_low = (probs * (prob_grad - mean_ref[...])).astype(BF16)
        value_term = dot(probs.astype(BF16), out_grads[...], 1, 0)
        key_term = dot(grad_low, queries[...], 1, 0) * SCALE
        dq_acc[...] += dot(keys, grad_low, 0, 0)
        return key_term, value_term

    def core_copy(ypos, half):
        place = pl.ds(2 * half, 2)
        return remote(
            dkv.at[ypos, place], core_rx.at[ypos, place], dc_send.at[ypos, half],
            dc_recv.at[ypos, half], at_core,
        )

    def y_copy(ypos, sender, half, device):
        place = pl.ds(2 * half, 2)
        return remote(
            y_sum.at[ypos, place], y_rx.at[sender, place], dy_send.at[ypos, half],
            dy_recv.at[sender, half], device,
        )

    def y_total(half):
        place = pl.ds(2 * half, 2)
        for step in (1, 2, 3):
            ypos, device = at_y(step)
            y_copy(ypos, ypos, half, device).wait_recv()
        total = y_sum[y, place].astype(F32)
        for step in (1, 2, 3):
            total = total + y_rx[(y + step) % NY, place].astype(F32)
        z_sum[place] = total.astype(BF16)

    def z_copy(zpos, part, place):
        return remote(
            z_sum.at[zpos, part], z_rx.at[zs, xl], dz_send.at[place], dz_recv.at[zs, xl],
            {"outer": z0 + zpos, "head": part},
        )

    def wait_z(zpos, part):
        remote(
            z_sum.at[zpos, part], z_rx.at[zpos, part], dz_send.at[0], dz_recv.at[zpos, part],
            {"outer": z0 + zpos, "head": part},
        ).wait_recv()

    far_places = [(2 * (1 - zq) + place // 2, place % 2, place) for place in range(4)]
    near = 4 * zq + 1 - zs
    near_places = [(near, 0, 4), (near, 1, 5), (zs, 1 - xl, 6)]

    def grad_place(turn):
        late, slot = turn % 2, turn // 2
        half = (1 - late) * (1 - zq) + late * zq
        ystep = ((1 - slot // 2) * (2 - slot) + slot // 2 * (slot + 1)) % NY
        return half, slot, at_y(ystep)

    def put_other(ypos, half, terms):
        place = pl.ds(2 * half, 2)
        for kind, term in enumerate(terms):
            dkv[ypos, place, :, kind] = term.astype(BF16).reshape(2, 2, ROWS, DH)
        core_copy(ypos, half).start()

    def put_own(ypos, half, terms):
        place = pl.ds(2 * half, 2)
        core_copy(ypos, half).wait_recv()
        for kind, term in enumerate(terms):
            total = term.reshape(2, 2, ROWS, DH) + core_rx[ypos, place, :, kind].astype(F32)
            y_sum[ypos, place, :, kind] = total.astype(BF16)

    def grad_step(index, carry):
        own = 1 - index % 2 - (1 - (index + 14) // 15) + index // 15
        half, slot, (ypos, device) = grad_place((index + 1) // 2 - own)

        @pl.when(index == 15)
        def far_sums():
            y_total(1 - zq)
            for far in far_places:
                z_copy(*far).start()

        terms = grad_block(ypos, 1 - c + own * (2 * c - 1), half)

        @pl.when(own == 0)
        def pass_on():
            put_other(ypos, half, terms)

        @pl.when(own == 1)
        def keep():
            put_own(ypos, half, terms)

            @pl.when(slot < NY - 1)
            def send():
                y_copy(ypos, y, half, device).start()

        return carry

    lax.fori_loop(0, 4 * NY, grad_step, 0)

    for pair in (1, 0):
        done = (dq_acc[:, pl.ds(pair * PAIR, PAIR)] * SCALE).T.astype(BF16)
        dq_stage[pair] = done.reshape(2, GROUP, ROWS, DH)
        for place, (of_pair, other) in enumerate(x_partners):
            if of_pair == pair:
                begin(
                    remote(
                        dq_stage.at[pair, other], dq_rx.at[pair, xh], dq_send.at[place],
                        dq_recv.at[pair, xh], at_x(pair, other),
                    )
                )
    dq_rx[1, xh] = dq_stage[1, xh]
    y_total(zq)
    for near_place in near_places:
        z_copy(*near_place).start()
    z_rx[zs, xl] = z_sum[zs, xl]
    for step in (2, 3, 1):
        for part in range(2):
            wait_z(at_z(step)[0], part)
    wait_z(zs, 1 - xl)
    for head in range(HK):
        total = z_rx[0, head].astype(F32)
        for zpos in range(1, NZ):
            total = total + z_rx[zpos, head].astype(F32)
        dk_out[:, pl.ds(head * DH, DH)] = total[0].astype(BF16)
        dv_out[:, pl.ds(head * DH, DH)] = total[1].astype(BF16)

    for pair, other in x_partners:
        remote(
            dq_stage.at[0, 0], dq_rx.at[pair, other], dq_send.at[0], dq_recv.at[pair, other],
            at_x(pair, other),
        ).wait_recv()
    for head in range(HQ):
        group, place = head // GROUP, head % GROUP
        pair = (xl + group + 1) % 2
        both = dq_rx[pair, 0, place].astype(F32) + dq_rx[pair, 1, place].astype(F32)
        dq_out[:, pl.ds(head * DH, DH)] = both.astype(BF16)

    for copy in sends:
        copy.wait_send()
    swap.wait_send()
    for kind in range(3):
        stat_copy(kind).wait_send()
    block_copy((y + 2) % NY, c).wait_send()
    for place in far_places + near_places:
        z_copy(*place).wait_send()
    for half in range(2):
        for ypos in range(NY):
            core_copy(ypos, half).wait_send()
        for step in (1, 2, 3):
            ypos, device = at_y(step)
            y_copy(ypos, y, half, device).wait_send()


def on_device(query, key, value, grad_out):
    vmem = pl.BlockSpec(memory_space=pltpu.VMEM)
    dma = pltpu.SemaphoreType.DMA
    rows = query.shape[0]
    return pl.pallas_call(
        kernel,
        out_shape=(
            pltpu.VMEM(query.shape, BF16),
            pltpu.VMEM(key.shape, BF16),
            pltpu.VMEM(value.shape, BF16),
        ),
        in_specs=[pl.BlockSpec(memory_space=pl.ANY)] * 4,
        out_specs=(vmem,) * 3,
        scratch_shapes=[
            pltpu.VMEM((rows, HQ * DH), BF16),
            pltpu.VMEM((rows, HK * DH), BF16),
            pltpu.VMEM((rows, HK * DH), BF16),
            pltpu.VMEM((rows, HQ * DH), BF16),
            pltpu.VMEM((HK, 2, GROUP, ROWS, DH), BF16),
            pltpu.VMEM((2, ROWS, DH), BF16),
            pltpu.VMEM((2, 2, 2, GROUP, ROWS, DH), BF16),
            pltpu.VMEM((NY, 2, NZ, 2, 2, ROWS, DH), BF16),
            pltpu.VMEM((NY, 2, BLOCK, QROWS), BF16),
            pltpu.VMEM((NY, 2, 1, QROWS), F32),
            pltpu.VMEM((1, QROWS), F32),
            pltpu.VMEM((1, QROWS), F32),
            pltpu.VMEM((1, QROWS), F32),
            pltpu.VMEM((1, QROWS), F32),
            pltpu.VMEM((1, QROWS), F32),
            pltpu.VMEM((1, QROWS), F32),
            pltpu.VMEM((1, QROWS), F32),
            pltpu.VMEM((1, QROWS), F32),
            pltpu.VMEM((DH, QROWS), F32),
            pltpu.VMEM((NY, NZ, 2, 2, ROWS, DH), BF16),
            pltpu.VMEM((NY, NZ, 2, 2, ROWS, DH), BF16),
            pltpu.VMEM((NY, NZ, 2, 2, ROWS, DH), BF16),
            pltpu.VMEM((NY, NZ, 2, 2, ROWS, DH), BF16),
            pltpu.VMEM((NZ, 2, 2, ROWS, DH), BF16),
            pltpu.VMEM((NZ, 2, 2, ROWS, DH), BF16),
            pltpu.VMEM((2, 2, GROUP, ROWS, DH), BF16),
            pltpu.VMEM((2, 2, GROUP, ROWS, DH), BF16),
            dma((4,)),
            dma((3,)),
            dma((2, 2)),
            dma((NZ, 2)),
            dma((NZ, 2)),
            dma((2, NZ)),
            dma((NZ,)),
            dma((NY, NZ)),
            dma((NY,)),
            dma((NY, 2)),
            dma((3,)),
            dma((3,)),
            dma((NY, 2)),
            dma((NY, 2)),
            dma((NY, 2)),
            dma((NY, 2)),
            dma((7,)),
            dma((NZ, 2)),
            dma((3,)),
            dma((2, 2)),
        ],
        compiler_params=pltpu.CompilerParams(
            collective_id=0, has_side_effects=True, vmem_limit_bytes=60 * 2**20
        ),
    )(query, key, value, grad_out)

def solution(mesh):
    spec = P(("head", "inner", "outer"), None)
    return jax.shard_map(
        on_device, mesh=mesh, in_specs=(spec,) * 4, out_specs=(spec,) * 3, check_vma=False
    )
```

```python
import functools
import math

import jax
import jax.numpy as jnp
from jax import lax
from jax.experimental import pallas as pl
from jax.experimental.pallas import tpu as pltpu
from jax.sharding import PartitionSpec as P

HQ = 14
HK = 2
DH = 128
ROWS = 64
GROUP = HQ // HK
NX = 4
NY = 4
NZ = 4
PAIR = 2 * GROUP * ROWS
QROWS = 2 * PAIR
BLOCK = NZ * 2 * ROWS
HALF = 2 * 2 * ROWS
SCALE = 1.0 / math.sqrt(DH)
SCALE2 = SCALE * math.log2(math.e)
F32 = jnp.float32
BF16 = jnp.bfloat16


def dot(left, right, left_dim, right_dim):
    return lax.dot_general(
        left, right, (((left_dim,), (right_dim,)), ((), ())), preferred_element_type=F32
    )


def kernel(
    q_in, k_in, v_in, g_in, dq_out, dk_out, dv_out,
    q_buf, k_buf, v_buf, g_buf,
    qg_stage, kv_stage, qg_all, kv_all, e_ref, mb_ref, m_ref, l_ref, d_ref, m_other, l_other, d_other, lse_ref, mean_ref,
    dq_acc, terms, dkv, core_rx, y_sum, y_rx, z_sum, z_rx, dq_stage, dq_rx,
    in_sem, qg_send, qg_recv, z_send, piece_recv, y_send, f_send, chunk_recv, c_send, c_recv,
    stat_send, stat_recv, dc_send, dc_recv, dy_send, dy_recv, dz_send, dz_recv,
    dq_send, dq_recv,
):
    xl = lax.axis_index("head")
    inner = lax.axis_index("inner")
    outer = lax.axis_index("outer")
    y = inner // 4
    xh = (inner // 2) % 2
    c = inner % 2
    zs = outer % NZ
    z0 = outer - zs
    zq = zs // 2

    def at_x(pair, other):
        return {"inner": 4 * y + 2 * other + c, "head": (xl + 1 - pair) % 2}

    def at_y(step):
        other = (y + step) % NY
        return other, {"inner": 4 * other + 2 * xh + c}

    def at_z(step):
        other = (zs + step) % NZ
        return other, {"outer": z0 + other}

    at_core = {"inner": 4 * y + 2 * xh + 1 - c}
    at_swap = {"head": 1 - xl}
    at_half = {"inner": 4 * y + 2 * (1 - xh) + c}

    def remote(src, dst, send_sem, recv_sem, device):
        return pltpu.make_async_remote_copy(
            src_ref=src, dst_ref=dst, send_sem=send_sem, recv_sem=recv_sem,
            device_id=device, device_id_type=pl.DeviceIdType.MESH,
        )

    barrier = pltpu.get_barrier_semaphore()
    x_partners = [(0, xh), (0, 1 - xh), (1, 1 - xh)]
    partners = [at_x(*place) for place in x_partners]
    partners += [at(step)[1] for at in (at_y, at_z) for step in (1, 2, 3)] + [at_core]
    partners += [{**at_z(step)[1], **at_swap} for step in (1, 2, 3)]
    for device in partners:
        pl.semaphore_signal(barrier, inc=1, device_id=device, device_id_type=pl.DeviceIdType.MESH)

    loads = [
        pltpu.make_async_copy(src, dst, in_sem.at[place])
        for place, (src, dst) in enumerate(
            [(k_in, k_buf), (v_in, v_buf), (q_in, q_buf), (g_in, g_buf)]
        )
    ]
    for load in loads:
        load.start()
    mine = pl.ds(pl.multiple_of(xl * DH, DH), DH)
    theirs = pl.ds(pl.multiple_of((1 - xl) * DH, DH), DH)
    loads[0].wait()
    kv_stage[0] = k_buf[:, theirs]
    kv_all[y, c, zs, xl, 0] = k_buf[:, mine]
    loads[1].wait()
    kv_stage[1] = v_buf[:, theirs]
    kv_all[y, c, zs, xl, 1] = v_buf[:, mine]
    pl.semaphore_wait(barrier, len(partners))

    sends = []

    def begin(copy):
        copy.start()
        sends.append(copy)

    def piece_copy(src, zpos, part, send_sem, device):
        return remote(src, kv_all.at[y, c, zpos, part], send_sem, piece_recv.at[zpos, part], device)

    swap = piece_copy(kv_stage, zs, xl, z_send.at[0, 0], at_swap)
    swap.start()
    for step in (1, 3, 2):
        begin(piece_copy(kv_all.at[y, c, zs, xl], zs, xl, z_send.at[step, 0], at_z(step)[1]))

    def query_copy(place):
        pair, other = x_partners[place]
        return remote(
            qg_stage.at[(xl + 1 - pair) % 2], qg_all.at[:, pair, xh], qg_send.at[place],
            qg_recv.at[pair, xh], at_x(pair, other),
        )

    def wait_queries(place):
        pair, other = x_partners[place]
        remote(
            qg_stage.at[0], qg_all.at[:, pair, other], qg_send.at[place], qg_recv.at[pair, other],
            at_x(pair, other),
        ).wait_recv()

    loads[2].wait()
    loads[3].wait()
    for head in range(HQ):
        columns = pl.ds(head * DH, DH)
        qg_stage[head // GROUP, 0, head % GROUP] = q_buf[:, columns]
        qg_stage[head // GROUP, 1, head % GROUP] = g_buf[:, columns]
    begin(query_copy(0))
    begin(query_copy(1))
    qg_all[:, 1, xh] = qg_stage[xl]

    def chunk_copy(ypos, zpos, send_sem, device):
        place = kv_all.at[ypos, c, zpos]
        return remote(place, place, send_sem, chunk_recv.at[ypos, zpos], device)

    def block_copy(ypos, core):
        place = kv_all.at[ypos, core]
        return remote(place, place, c_send.at[ypos], c_recv.at[ypos, core], at_core)

    def forward_copy(step):
        ystep, target = (1, 3) if step < 2 else (3, 1)
        return chunk_copy(
            (y + ystep) % NY, (zs + step) % NZ, f_send.at[step], at_y(target)[1]
        )

    piece_copy(kv_stage, zs, 1 - xl, z_send.at[0, 0], at_swap).wait_recv()
    for step in (1, 3, 2):
        place = kv_all.at[y, c, zs, 1 - xl]
        begin(piece_copy(place, zs, 1 - xl, z_send.at[step, 1], at_z(step)[1]))
    for step in (0, 1, 3, 2):
        zpos, device = at_z(step)
        if step:
            for part in (xl, 1 - xl):
                piece_copy(kv_stage, zpos, part, z_send.at[0, 0], device).wait_recv()
        for place, ystep in enumerate((1, 3)):
            begin(chunk_copy(y, zpos, y_send.at[place, step], at_y(ystep)[1]))
        if step == 0:
            begin(query_copy(2))
    begin(block_copy(y, c))

    def wait_chunk(ystep, step):
        ypos, device = at_y(ystep)
        chunk_copy(ypos, (zs + step) % NZ, y_send.at[0, 0], device).wait_recv()

    for step in (0, 1, 3, 2):
        for ystep in (1, 3):
            wait_chunk(ystep, step)
            if (step < 2) == (ystep == 1):
                begin(forward_copy(step))
    for ystep in (1, 3):
        begin(block_copy((y + ystep) % NY, c))
    for place in range(3):
        wait_queries(place)

    queries = qg_all.at[0].reshape(QROWS, DH)
    out_grads = qg_all.at[1].reshape(QROWS, DH)

    stats = [(m_ref, m_other), (l_ref, l_other), (d_ref, d_other)]

    def stat_copy(kind):
        own, other = stats[kind]
        return remote(own, other, stat_send.at[kind], stat_recv.at[kind], at_half)

    def wait_core(ystep):
        block_copy((y + ystep) % NY, 1 - c).wait_recv()

    m_ref[...] = jnp.full_like(m_ref, -1e30)
    l_ref[...] = jnp.zeros_like(l_ref)
    d_ref[...] = jnp.zeros_like(d_ref)

    def stats_step(turn, carry):
        @pl.when(turn == 1)
        def first():
            wait_core(0)

        @pl.when(turn == 3)
        def second():
            wait_core(1)

        @pl.when(turn == 4)
        def opposite():
            for step in range(NZ):
                wait_chunk(2, step)
            block_copy((y + 2) % NY, c).start()

        @pl.when(turn == 5)
        def third():
            wait_core(3)

        @pl.when(turn == 7)
        def last():
            wait_core(2)

        slot, role = turn // 2, turn % 2
        ypos = (y + slot + slot // 2 - 2 * (slot // 3)) % NY
        core = c + role * (1 - 2 * c)
        keys = kv_all[ypos, core, :, :, 0].reshape(BLOCK, DH)
        values = kv_all[ypos, core, :, :, 1].reshape(BLOCK, DH)
        scores = dot(keys, queries[...], 1, 1)
        prob_grad = dot(values, out_grads[...], 1, 1)
        old = m_ref[...]
        new = jnp.maximum(old, jnp.max(scores, axis=0, keepdims=True) * SCALE2)
        factor = jnp.exp2(old - new)
        weights = jnp.exp2(scores * SCALE2 - new)
        e_ref[ypos, core] = weights.astype(BF16)
        mb_ref[ypos, core] = new
        m_ref[...] = new
        l_ref[...] = l_ref[...] * factor + jnp.sum(weights, axis=0, keepdims=True)
        d_ref[...] = d_ref[...] * factor + jnp.sum(weights * prob_grad, axis=0, keepdims=True)
        return carry

    lax.fori_loop(0, 2 * NY, stats_step, 0)

    for kind in range(3):
        stat_copy(kind).start()
    dq_acc[...] = jnp.zeros_like(dq_acc)
    for kind in range(3):
        stat_copy(kind).wait_recv()
    top = jnp.maximum(m_ref[...], m_other[...])
    own_factor = jnp.exp2(m_ref[...] - top)
    other_factor = jnp.exp2(m_other[...] - top)
    total = l_ref[...] * own_factor + l_other[...] * other_factor
    weighted = d_ref[...] * own_factor + d_other[...] * other_factor
    lse_ref[...] = top + jnp.log2(total)
    mean_ref[...] = weighted / total

    def grad_block(ypos, half):
        keys = kv_all[ypos, :, pl.ds(2 * half, 2), :, 0].reshape(2 * HALF, DH)
        values = kv_all[ypos, :, pl.ds(2 * half, 2), :, 1].reshape(2 * HALF, DH)
        prob_grad = dot(values, out_grads[...], 1, 1)
        place = pl.ds(pl.multiple_of(half * HALF, HALF), HALF)
        probs = jnp.concatenate(
            [
                e_ref[ypos, core, place, :].astype(F32)
                * jnp.exp2(mb_ref[ypos, core] - lse_ref[...])
                for core in range(2)
            ],
            axis=0,
        )
        grad_low = (probs * (prob_grad - mean_ref[...])).astype(BF16)
        value_term = dot(probs.astype(BF16), out_grads[...], 1, 0)
        key_term = dot(grad_low, queries[...], 1, 0) * SCALE
        dq_acc[...] += dot(keys, grad_low, 0, 0)
        shape = (2, 2, 2, ROWS, DH)
        return key_term.reshape(shape), value_term.reshape(shape)

    def core_copy(ypos, half):
        place = pl.ds(2 * half, 2)
        return remote(
            dkv.at[ypos, place], core_rx.at[ypos, place], dc_send.at[ypos, half],
            dc_recv.at[ypos, half], at_core,
        )

    def y_copy(ypos, sender, half, device):
        place = pl.ds(2 * half, 2)
        return remote(
            y_sum.at[ypos, place], y_rx.at[sender, place], dy_send.at[ypos, half],
            dy_recv.at[sender, half], device,
        )

    def y_total(half):
        place = pl.ds(2 * half, 2)
        for step in (1, 2, 3):
            ypos, device = at_y(step)
            y_copy(ypos, ypos, half, device).wait_recv()
        total = y_sum[y, place].astype(F32)
        for step in (1, 2, 3):
            total = total + y_rx[(y + step) % NY, place].astype(F32)
        z_sum[place] = total.astype(BF16)

    def z_copy(zpos, part, place):
        return remote(
            z_sum.at[zpos, part], z_rx.at[zs, xl], dz_send.at[place], dz_recv.at[zs, xl],
            {"outer": z0 + zpos, "head": part},
        )

    def wait_z(zpos, part):
        remote(
            z_sum.at[zpos, part], z_rx.at[zpos, part], dz_send.at[0], dz_recv.at[zpos, part],
            {"outer": z0 + zpos, "head": part},
        ).wait_recv()

    far_places = [(2 * (1 - zq) + place // 2, place % 2, place) for place in range(4)]
    near = 4 * zq + 1 - zs
    near_places = [(near, 0, 4), (near, 1, 5), (zs, 1 - xl, 6)]

    def grad_place(turn):
        late, slot = turn % 2, turn // 2
        half = (1 - late) * (1 - zq) + late * zq
        ystep = ((1 - slot // 2) * (2 - slot) + slot // 2 * (slot + 1)) % NY
        return half, slot, at_y(ystep)

    def put_other(turn):
        half, slot, (ypos, device) = grad_place(turn)
        for kind in range(2):
            dkv[ypos, pl.ds(2 * half, 2), :, kind] = terms[turn % 2, kind, 1 - c].astype(BF16)
        core_copy(ypos, half).start()

    def put_own(turn):
        half, slot, (ypos, device) = grad_place(turn)
        place = pl.ds(2 * half, 2)
        core_copy(ypos, half).wait_recv()
        for kind in range(2):
            total = terms[turn % 2, kind, c] + core_rx[ypos, place, :, kind].astype(F32)
            y_sum[ypos, place, :, kind] = total.astype(BF16)

        @pl.when(slot < NY - 1)
        def send():
            y_copy(ypos, y, half, device).start()

    def grad_step(turn, carry):
        half, slot, (ypos, device) = grad_place(turn)
        for kind, term in enumerate(grad_block(ypos, half)):
            terms[turn % 2, kind] = term
        put_other(turn)

        @pl.when(turn > 0)
        def last_turn():
            put_own(turn - 1)

        return carry

    lax.fori_loop(0, 2 * NY, grad_step, 0)
    y_total(1 - zq)
    for far in far_places:
        z_copy(*far).start()

    for pair in (1, 0):
        done = (dq_acc[:, pl.ds(pair * PAIR, PAIR)] * SCALE).T.astype(BF16)
        dq_stage[pair] = done.reshape(2, GROUP, ROWS, DH)
        for place, (of_pair, other) in enumerate(x_partners):
            if of_pair == pair:
                begin(
                    remote(
                        dq_stage.at[pair, other], dq_rx.at[pair, xh], dq_send.at[place],
                        dq_recv.at[pair, xh], at_x(pair, other),
                    )
                )
    dq_rx[1, xh] = dq_stage[1, xh]
    put_own(2 * NY - 1)
    y_total(zq)
    for near_place in near_places:
        z_copy(*near_place).start()
    z_rx[zs, xl] = z_sum[zs, xl]
    for step in (2, 3, 1):
        for part in range(2):
            wait_z(at_z(step)[0], part)
    wait_z(zs, 1 - xl)
    for head in range(HK):
        total = z_rx[0, head].astype(F32)
        for zpos in range(1, NZ):
            total = total + z_rx[zpos, head].astype(F32)
        dk_out[:, pl.ds(head * DH, DH)] = total[0].astype(BF16)
        dv_out[:, pl.ds(head * DH, DH)] = total[1].astype(BF16)

    for pair, other in x_partners:
        remote(
            dq_stage.at[0, 0], dq_rx.at[pair, other], dq_send.at[0], dq_recv.at[pair, other],
            at_x(pair, other),
        ).wait_recv()
    for head in range(HQ):
        group, place = head // GROUP, head % GROUP
        pair = (xl + group + 1) % 2
        both = dq_rx[pair, 0, place].astype(F32) + dq_rx[pair, 1, place].astype(F32)
        dq_out[:, pl.ds(head * DH, DH)] = both.astype(BF16)

    for copy in sends:
        copy.wait_send()
    swap.wait_send()
    for kind in range(3):
        stat_copy(kind).wait_send()
    block_copy((y + 2) % NY, c).wait_send()
    for place in far_places + near_places:
        z_copy(*place).wait_send()
    for half in range(2):
        for ypos in range(NY):
            core_copy(ypos, half).wait_send()
        for step in (1, 2, 3):
            ypos, device = at_y(step)
            y_copy(ypos, y, half, device).wait_send()


def on_device(query, key, value, grad_out):
    vmem = pl.BlockSpec(memory_space=pltpu.VMEM)
    dma = pltpu.SemaphoreType.DMA
    rows = query.shape[0]
    return pl.pallas_call(
        kernel,
        out_shape=(
            pltpu.VMEM(query.shape, BF16),
            pltpu.VMEM(key.shape, BF16),
            pltpu.VMEM(value.shape, BF16),
        ),
        in_specs=[pl.BlockSpec(memory_space=pl.ANY)] * 4,
        out_specs=(vmem,) * 3,
        scratch_shapes=[
            pltpu.VMEM((rows, HQ * DH), BF16),
            pltpu.VMEM((rows, HK * DH), BF16),
            pltpu.VMEM((rows, HK * DH), BF16),
            pltpu.VMEM((rows, HQ * DH), BF16),
            pltpu.VMEM((HK, 2, GROUP, ROWS, DH), BF16),
            pltpu.VMEM((2, ROWS, DH), BF16),
            pltpu.VMEM((2, 2, 2, GROUP, ROWS, DH), BF16),
            pltpu.VMEM((NY, 2, NZ, 2, 2, ROWS, DH), BF16),
            pltpu.VMEM((NY, 2, BLOCK, QROWS), BF16),
            pltpu.VMEM((NY, 2, 1, QROWS), F32),
            pltpu.VMEM((1, QROWS), F32),
            pltpu.VMEM((1, QROWS), F32),
            pltpu.VMEM((1, QROWS), F32),
            pltpu.VMEM((1, QROWS), F32),
            pltpu.VMEM((1, QROWS), F32),
            pltpu.VMEM((1, QROWS), F32),
            pltpu.VMEM((1, QROWS), F32),
            pltpu.VMEM((1, QROWS), F32),
            pltpu.VMEM((DH, QROWS), F32),
            pltpu.VMEM((2, 2, 2, 2, 2, ROWS, DH), F32),
            pltpu.VMEM((NY, NZ, 2, 2, ROWS, DH), BF16),
            pltpu.VMEM((NY, NZ, 2, 2, ROWS, DH), BF16),
            pltpu.VMEM((NY, NZ, 2, 2, ROWS, DH), BF16),
            pltpu.VMEM((NY, NZ, 2, 2, ROWS, DH), BF16),
            pltpu.VMEM((NZ, 2, 2, ROWS, DH), BF16),
            pltpu.VMEM((NZ, 2, 2, ROWS, DH), BF16),
            pltpu.VMEM((2, 2, GROUP, ROWS, DH), BF16),
            pltpu.VMEM((2, 2, GROUP, ROWS, DH), BF16),
            dma((4,)),
            dma((3,)),
            dma((2, 2)),
            dma((NZ, 2)),
            dma((NZ, 2)),
            dma((2, NZ)),
            dma((NZ,)),
            dma((NY, NZ)),
            dma((NY,)),
            dma((NY, 2)),
            dma((3,)),
            dma((3,)),
            dma((NY, 2)),
            dma((NY, 2)),
            dma((NY, 2)),
            dma((NY, 2)),
            dma((7,)),
            dma((NZ, 2)),
            dma((3,)),
            dma((2, 2)),
        ],
        compiler_params=pltpu.CompilerParams(
            collective_id=0, has_side_effects=True, vmem_limit_bytes=60 * 2**20
        ),
    )(query, key, value, grad_out)

def solution(mesh):
    spec = P(("head", "inner", "outer"), None)
    return jax.shard_map(
        on_device, mesh=mesh, in_specs=(spec,) * 4, out_specs=(spec,) * 3, check_vma=False
    )
```

```python
import functools
import math

import jax
import jax.numpy as jnp
from jax import lax
from jax.experimental import pallas as pl
from jax.experimental.pallas import tpu as pltpu
from jax.sharding import PartitionSpec as P

HQ = 14
HK = 2
DH = 128
ROWS = 64
GROUP = HQ // HK
NX = 4
NY = 4
NZ = 4
PAIR = 2 * GROUP * ROWS
QROWS = 2 * PAIR
BLOCK = 2 * NZ * 2 * ROWS
HALF = 2 * 2 * ROWS
SCALE = 1.0 / math.sqrt(DH)
SCALE2 = SCALE * math.log2(math.e)
F32 = jnp.float32
BF16 = jnp.bfloat16


def dot(left, right, left_dim, right_dim):
    return lax.dot_general(
        left, right, (((left_dim,), (right_dim,)), ((), ())), preferred_element_type=F32
    )


def kernel(
    q_in, k_in, v_in, g_in, dq_out, dk_out, dv_out,
    q_buf, k_buf, v_buf, g_buf,
    qg_stage, kv_stage, qg_all, kv_all, e_ref, mb_ref, m_ref, l_ref, d_ref, m_other, l_other, d_other, lse_ref, mean_ref,
    dq_acc, terms, dkv, core_rx, y_sum, y_rx, z_sum, z_rx, dq_stage, dq_rx,
    in_sem, qg_send, qg_recv, z_send, piece_recv, y_send, f_send, chunk_recv, c_send, c_recv,
    stat_send, stat_recv, dc_send, dc_recv, dy_send, dy_recv, dz_send, dz_recv,
    dq_send, dq_recv,
):
    xl = lax.axis_index("head")
    inner = lax.axis_index("inner")
    outer = lax.axis_index("outer")
    y = inner // 4
    xh = (inner // 2) % 2
    c = inner % 2
    zs = outer % NZ
    z0 = outer - zs
    zq = zs // 2

    def at_x(pair, other):
        return {"inner": 4 * y + 2 * other + c, "head": (xl + 1 - pair) % 2}

    def at_y(step):
        other = (y + step) % NY
        return other, {"inner": 4 * other + 2 * xh + c}

    def at_z(step):
        other = (zs + step) % NZ
        return other, {"outer": z0 + other}

    at_core = {"inner": 4 * y + 2 * xh + 1 - c}
    at_swap = {"head": 1 - xl}
    at_half = {"inner": 4 * y + 2 * (1 - xh) + c}

    def remote(src, dst, send_sem, recv_sem, device):
        return pltpu.make_async_remote_copy(
            src_ref=src, dst_ref=dst, send_sem=send_sem, recv_sem=recv_sem,
            device_id=device, device_id_type=pl.DeviceIdType.MESH,
        )

    barrier = pltpu.get_barrier_semaphore()
    x_partners = [(0, xh), (0, 1 - xh), (1, 1 - xh)]
    partners = [at_x(*place) for place in x_partners]
    partners += [at(step)[1] for at in (at_y, at_z) for step in (1, 2, 3)] + [at_core]
    partners += [{**at_z(step)[1], **at_swap} for step in (1, 2, 3)]
    for device in partners:
        pl.semaphore_signal(barrier, inc=1, device_id=device, device_id_type=pl.DeviceIdType.MESH)

    loads = [
        pltpu.make_async_copy(src, dst, in_sem.at[place])
        for place, (src, dst) in enumerate(
            [(k_in, k_buf), (v_in, v_buf), (q_in, q_buf), (g_in, g_buf)]
        )
    ]
    for load in loads:
        load.start()
    mine = pl.ds(pl.multiple_of(xl * DH, DH), DH)
    theirs = pl.ds(pl.multiple_of((1 - xl) * DH, DH), DH)
    loads[0].wait()
    kv_stage[0] = k_buf[:, theirs]
    kv_all[y, c, zs, xl, 0] = k_buf[:, mine]
    loads[1].wait()
    kv_stage[1] = v_buf[:, theirs]
    kv_all[y, c, zs, xl, 1] = v_buf[:, mine]
    pl.semaphore_wait(barrier, len(partners))

    sends = []

    def begin(copy):
        copy.start()
        sends.append(copy)

    def piece_copy(src, zpos, part, send_sem, device):
        return remote(src, kv_all.at[y, c, zpos, part], send_sem, piece_recv.at[zpos, part], device)

    swap = piece_copy(kv_stage, zs, xl, z_send.at[0, 0], at_swap)
    swap.start()
    for step in (1, 3, 2):
        begin(piece_copy(kv_all.at[y, c, zs, xl], zs, xl, z_send.at[step, 0], at_z(step)[1]))

    def query_copy(place):
        pair, other = x_partners[place]
        return remote(
            qg_stage.at[(xl + 1 - pair) % 2], qg_all.at[:, pair, xh], qg_send.at[place],
            qg_recv.at[pair, xh], at_x(pair, other),
        )

    def wait_queries(place):
        pair, other = x_partners[place]
        remote(
            qg_stage.at[0], qg_all.at[:, pair, other], qg_send.at[place], qg_recv.at[pair, other],
            at_x(pair, other),
        ).wait_recv()

    loads[2].wait()
    loads[3].wait()
    for head in range(HQ):
        columns = pl.ds(head * DH, DH)
        qg_stage[head // GROUP, 0, head % GROUP] = q_buf[:, columns]
        qg_stage[head // GROUP, 1, head % GROUP] = g_buf[:, columns]
    begin(query_copy(0))
    begin(query_copy(1))
    qg_all[:, 1, xh] = qg_stage[xl]

    def chunk_copy(ypos, zpos, send_sem, device):
        place = kv_all.at[ypos, c, zpos]
        return remote(place, place, send_sem, chunk_recv.at[ypos, zpos], device)

    def block_copy(ypos, core):
        place = kv_all.at[ypos, core]
        return remote(place, place, c_send.at[ypos], c_recv.at[ypos, core], at_core)

    def forward_copy(step):
        ystep, target = (1, 3) if step < 2 else (3, 1)
        return chunk_copy(
            (y + ystep) % NY, (zs + step) % NZ, f_send.at[step], at_y(target)[1]
        )

    piece_copy(kv_stage, zs, 1 - xl, z_send.at[0, 0], at_swap).wait_recv()
    for step in (1, 3, 2):
        place = kv_all.at[y, c, zs, 1 - xl]
        begin(piece_copy(place, zs, 1 - xl, z_send.at[step, 1], at_z(step)[1]))
    for step in (0, 1, 3, 2):
        zpos, device = at_z(step)
        if step:
            for part in (xl, 1 - xl):
                piece_copy(kv_stage, zpos, part, z_send.at[0, 0], device).wait_recv()
        for place, ystep in enumerate((1, 3)):
            begin(chunk_copy(y, zpos, y_send.at[place, step], at_y(ystep)[1]))
        if step == 0:
            begin(query_copy(2))
    begin(block_copy(y, c))

    def wait_chunk(ystep, step):
        ypos, device = at_y(ystep)
        chunk_copy(ypos, (zs + step) % NZ, y_send.at[0, 0], device).wait_recv()

    for step in (0, 1, 3, 2):
        for ystep in (1, 3):
            wait_chunk(ystep, step)
            if (step < 2) == (ystep == 1):
                begin(forward_copy(step))
    for ystep in (1, 3):
        begin(block_copy((y + ystep) % NY, c))
    for place in range(3):
        wait_queries(place)

    queries = qg_all.at[0].reshape(QROWS, DH)
    out_grads = qg_all.at[1].reshape(QROWS, DH)

    stats = [(m_ref, m_other), (l_ref, l_other), (d_ref, d_other)]

    def stat_copy(kind):
        own, other = stats[kind]
        return remote(own, other, stat_send.at[kind], stat_recv.at[kind], at_half)

    def wait_core(ystep):
        block_copy((y + ystep) % NY, 1 - c).wait_recv()

    m_ref[...] = jnp.full_like(m_ref, -1e30)
    l_ref[...] = jnp.zeros_like(l_ref)
    d_ref[...] = jnp.zeros_like(d_ref)

    def stats_step(turn, carry):
        @pl.when(turn == 1)
        def second():
            wait_core(1)

        @pl.when(turn == 2)
        def third():
            for step in range(NZ):
                wait_chunk(2, step)
            block_copy((y + 2) % NY, c).start()
            wait_core(3)

        @pl.when(turn == 3)
        def last():
            wait_core(2)

        ypos = (y + turn + turn // 2 - 2 * (turn // 3)) % NY
        keys = kv_all[ypos, :, :, :, 0].reshape(BLOCK, DH)
        values = kv_all[ypos, :, :, :, 1].reshape(BLOCK, DH)
        scores = dot(keys, queries[...], 1, 1)
        prob_grad = dot(values, out_grads[...], 1, 1)
        old = m_ref[...]
        new = jnp.maximum(old, jnp.max(scores, axis=0, keepdims=True) * SCALE2)
        factor = jnp.exp2(old - new)
        weights = jnp.exp2(scores * SCALE2 - new)
        e_ref[ypos] = weights.astype(BF16).reshape(2, BLOCK // 2, QROWS)
        mb_ref[ypos] = new
        m_ref[...] = new
        l_ref[...] = l_ref[...] * factor + jnp.sum(weights, axis=0, keepdims=True)
        d_ref[...] = d_ref[...] * factor + jnp.sum(weights * prob_grad, axis=0, keepdims=True)
        return carry

    wait_core(0)
    lax.fori_loop(0, NY, stats_step, 0)

    for kind in range(3):
        stat_copy(kind).start()
    dq_acc[...] = jnp.zeros_like(dq_acc)
    for kind in range(3):
        stat_copy(kind).wait_recv()
    top = jnp.maximum(m_ref[...], m_other[...])
    own_factor = jnp.exp2(m_ref[...] - top)
    other_factor = jnp.exp2(m_other[...] - top)
    total = l_ref[...] * own_factor + l_other[...] * other_factor
    weighted = d_ref[...] * own_factor + d_other[...] * other_factor
    lse_ref[...] = top + jnp.log2(total)
    mean_ref[...] = weighted / total

    def grad_block(ypos, half):
        keys = kv_all[ypos, :, pl.ds(2 * half, 2), :, 0].reshape(2 * HALF, DH)
        values = kv_all[ypos, :, pl.ds(2 * half, 2), :, 1].reshape(2 * HALF, DH)
        prob_grad = dot(values, out_grads[...], 1, 1)
        place = pl.ds(pl.multiple_of(half * HALF, HALF), HALF)
        factor = jnp.exp2(mb_ref[ypos] - lse_ref[...])
        probs = e_ref[ypos, :, place, :].reshape(2 * HALF, QROWS).astype(F32) * factor
        grad_low = (probs * (prob_grad - mean_ref[...])).astype(BF16)
        value_term = dot(probs.astype(BF16), out_grads[...], 1, 0)
        key_term = dot(grad_low, queries[...], 1, 0) * SCALE
        dq_acc[...] += dot(keys, grad_low, 0, 0)
        shape = (2, 2, 2, ROWS, DH)
        return key_term.reshape(shape), value_term.reshape(shape)

    def core_copy(ypos, half):
        place = pl.ds(2 * half, 2)
        return remote(
            dkv.at[ypos, place], core_rx.at[ypos, place], dc_send.at[ypos, half],
            dc_recv.at[ypos, half], at_core,
        )

    def y_copy(ypos, sender, half, device):
        place = pl.ds(2 * half, 2)
        return remote(
            y_sum.at[ypos, place], y_rx.at[sender, place], dy_send.at[ypos, half],
            dy_recv.at[sender, half], device,
        )

    def y_total(half):
        place = pl.ds(2 * half, 2)
        for step in (1, 2, 3):
            ypos, device = at_y(step)
            y_copy(ypos, ypos, half, device).wait_recv()
        total = y_sum[y, place].astype(F32)
        for step in (1, 2, 3):
            total = total + y_rx[(y + step) % NY, place].astype(F32)
        z_sum[place] = total.astype(BF16)

    def z_copy(zpos, part, place):
        return remote(
            z_sum.at[zpos, part], z_rx.at[zs, xl], dz_send.at[place], dz_recv.at[zs, xl],
            {"outer": z0 + zpos, "head": part},
        )

    def wait_z(zpos, part):
        remote(
            z_sum.at[zpos, part], z_rx.at[zpos, part], dz_send.at[0], dz_recv.at[zpos, part],
            {"outer": z0 + zpos, "head": part},
        ).wait_recv()

    far_places = [(2 * (1 - zq) + place // 2, place % 2, place) for place in range(4)]
    near = 4 * zq + 1 - zs
    near_places = [(near, 0, 4), (near, 1, 5), (zs, 1 - xl, 6)]

    def grad_place(turn):
        late, slot = turn % 2, turn // 2
        half = (1 - late) * (1 - zq) + late * zq
        ystep = ((1 - slot // 2) * (2 - slot) + slot // 2 * (slot + 1)) % NY
        return half, slot, at_y(ystep)

    def put_other(turn):
        half, slot, (ypos, device) = grad_place(turn)
        for kind in range(2):
            dkv[ypos, pl.ds(2 * half, 2), :, kind] = terms[turn % 2, kind, 1 - c].astype(BF16)
        core_copy(ypos, half).start()

    def put_own(turn):
        half, slot, (ypos, device) = grad_place(turn)
        place = pl.ds(2 * half, 2)
        core_copy(ypos, half).wait_recv()
        for kind in range(2):
            total = terms[turn % 2, kind, c] + core_rx[ypos, place, :, kind].astype(F32)
            y_sum[ypos, place, :, kind] = total.astype(BF16)

        @pl.when(slot < NY - 1)
        def send():
            y_copy(ypos, y, half, device).start()

    def grad_step(turn, carry):
        half, slot, (ypos, device) = grad_place(turn)
        for kind, term in enumerate(grad_block(ypos, half)):
            terms[turn % 2, kind] = term
        put_other(turn)

        @pl.when(turn > 0)
        def last_turn():
            put_own(turn - 1)

        return carry

    lax.fori_loop(0, 2 * NY, grad_step, 0)
    y_total(1 - zq)
    for far in far_places:
        z_copy(*far).start()

    for pair in (1, 0):
        done = (dq_acc[:, pl.ds(pair * PAIR, PAIR)] * SCALE).T.astype(BF16)
        dq_stage[pair] = done.reshape(2, GROUP, ROWS, DH)
        for place, (of_pair, other) in enumerate(x_partners):
            if of_pair == pair:
                begin(
                    remote(
                        dq_stage.at[pair, other], dq_rx.at[pair, xh], dq_send.at[place],
                        dq_recv.at[pair, xh], at_x(pair, other),
                    )
                )
    dq_rx[1, xh] = dq_stage[1, xh]
    put_own(2 * NY - 1)
    y_total(zq)
    for near_place in near_places:
        z_copy(*near_place).start()
    z_rx[zs, xl] = z_sum[zs, xl]
    for step in (2, 3, 1):
        for part in range(2):
            wait_z(at_z(step)[0], part)
    wait_z(zs, 1 - xl)
    for head in range(HK):
        total = z_rx[0, head].astype(F32)
        for zpos in range(1, NZ):
            total = total + z_rx[zpos, head].astype(F32)
        dk_out[:, pl.ds(head * DH, DH)] = total[0].astype(BF16)
        dv_out[:, pl.ds(head * DH, DH)] = total[1].astype(BF16)

    for pair, other in x_partners:
        remote(
            dq_stage.at[0, 0], dq_rx.at[pair, other], dq_send.at[0], dq_recv.at[pair, other],
            at_x(pair, other),
        ).wait_recv()
    for head in range(HQ):
        group, place = head // GROUP, head % GROUP
        pair = (xl + group + 1) % 2
        both = dq_rx[pair, 0, place].astype(F32) + dq_rx[pair, 1, place].astype(F32)
        dq_out[:, pl.ds(head * DH, DH)] = both.astype(BF16)

    for copy in sends:
        copy.wait_send()
    swap.wait_send()
    for kind in range(3):
        stat_copy(kind).wait_send()
    block_copy((y + 2) % NY, c).wait_send()
    for place in far_places + near_places:
        z_copy(*place).wait_send()
    for half in range(2):
        for ypos in range(NY):
            core_copy(ypos, half).wait_send()
        for step in (1, 2, 3):
            ypos, device = at_y(step)
            y_copy(ypos, y, half, device).wait_send()


def on_device(query, key, value, grad_out):
    vmem = pl.BlockSpec(memory_space=pltpu.VMEM)
    dma = pltpu.SemaphoreType.DMA
    rows = query.shape[0]
    return pl.pallas_call(
        kernel,
        out_shape=(
            pltpu.VMEM(query.shape, BF16),
            pltpu.VMEM(key.shape, BF16),
            pltpu.VMEM(value.shape, BF16),
        ),
        in_specs=[pl.BlockSpec(memory_space=pl.ANY)] * 4,
        out_specs=(vmem,) * 3,
        scratch_shapes=[
            pltpu.VMEM((rows, HQ * DH), BF16),
            pltpu.VMEM((rows, HK * DH), BF16),
            pltpu.VMEM((rows, HK * DH), BF16),
            pltpu.VMEM((rows, HQ * DH), BF16),
            pltpu.VMEM((HK, 2, GROUP, ROWS, DH), BF16),
            pltpu.VMEM((2, ROWS, DH), BF16),
            pltpu.VMEM((2, 2, 2, GROUP, ROWS, DH), BF16),
            pltpu.VMEM((NY, 2, NZ, 2, 2, ROWS, DH), BF16),
            pltpu.VMEM((NY, 2, BLOCK // 2, QROWS), BF16),
            pltpu.VMEM((NY, 1, QROWS), F32),
            pltpu.VMEM((1, QROWS), F32),
            pltpu.VMEM((1, QROWS), F32),
            pltpu.VMEM((1, QROWS), F32),
            pltpu.VMEM((1, QROWS), F32),
            pltpu.VMEM((1, QROWS), F32),
            pltpu.VMEM((1, QROWS), F32),
            pltpu.VMEM((1, QROWS), F32),
            pltpu.VMEM((1, QROWS), F32),
            pltpu.VMEM((DH, QROWS), F32),
            pltpu.VMEM((2, 2, 2, 2, 2, ROWS, DH), F32),
            pltpu.VMEM((NY, NZ, 2, 2, ROWS, DH), BF16),
            pltpu.VMEM((NY, NZ, 2, 2, ROWS, DH), BF16),
            pltpu.VMEM((NY, NZ, 2, 2, ROWS, DH), BF16),
            pltpu.VMEM((NY, NZ, 2, 2, ROWS, DH), BF16),
            pltpu.VMEM((NZ, 2, 2, ROWS, DH), BF16),
            pltpu.VMEM((NZ, 2, 2, ROWS, DH), BF16),
            pltpu.VMEM((2, 2, GROUP, ROWS, DH), BF16),
            pltpu.VMEM((2, 2, GROUP, ROWS, DH), BF16),
            dma((4,)),
            dma((3,)),
            dma((2, 2)),
            dma((NZ, 2)),
            dma((NZ, 2)),
            dma((2, NZ)),
            dma((NZ,)),
            dma((NY, NZ)),
            dma((NY,)),
            dma((NY, 2)),
            dma((3,)),
            dma((3,)),
            dma((NY, 2)),
            dma((NY, 2)),
            dma((NY, 2)),
            dma((NY, 2)),
            dma((7,)),
            dma((NZ, 2)),
            dma((3,)),
            dma((2, 2)),
        ],
        compiler_params=pltpu.CompilerParams(
            collective_id=0, has_side_effects=True, vmem_limit_bytes=60 * 2**20
        ),
    )(query, key, value, grad_out)

def solution(mesh):
    spec = P(("head", "inner", "outer"), None)
    return jax.shard_map(
        on_device, mesh=mesh, in_specs=(spec,) * 4, out_specs=(spec,) * 3, check_vma=False
    )
```

```python
import functools
import math

import jax
import jax.numpy as jnp
from jax import lax
from jax.experimental import pallas as pl
from jax.experimental.pallas import tpu as pltpu
from jax.sharding import PartitionSpec as P

HQ = 14
HK = 2
DH = 128
ROWS = 64
GROUP = HQ // HK
NX = 4
NY = 4
NZ = 4
PAIR = 2 * GROUP * ROWS
QROWS = 2 * PAIR
BLOCK = 2 * NZ * 2 * ROWS
HALF = 2 * 2 * ROWS
SCALE = 1.0 / math.sqrt(DH)
SCALE2 = SCALE * math.log2(math.e)
F32 = jnp.float32
BF16 = jnp.bfloat16


def dot(left, right, left_dim, right_dim):
    return lax.dot_general(
        left, right, (((left_dim,), (right_dim,)), ((), ())), preferred_element_type=F32
    )


def kernel(
    q_in, k_in, v_in, g_in, dq_out, dk_out, dv_out,
    q_buf, k_buf, v_buf, g_buf,
    qg_stage, kv_stage, qg_all, kv_all, e_ref, mb_ref, m_ref, l_ref, d_ref, m_other, l_other, d_other, lse_ref, mean_ref,
    dq_acc, terms, dkv, core_rx, y_sum, y_rx, z_sum, z_rx, dq_stage, dq_rx,
    in_sem, qg_send, qg_recv, z_send, piece_recv, y_send, f_send, chunk_recv, c_send, c_recv,
    stat_send, stat_recv, dc_send, dc_recv, dy_send, dy_recv, dz_send, dz_recv,
    dq_send, dq_recv,
):
    xl = lax.axis_index("head")
    inner = lax.axis_index("inner")
    outer = lax.axis_index("outer")
    y = inner // 4
    xh = (inner // 2) % 2
    c = inner % 2
    zs = outer % NZ
    z0 = outer - zs
    zq = zs // 2

    def at_x(pair, other):
        return {"inner": 4 * y + 2 * other + c, "head": (xl + 1 - pair) % 2}

    def at_y(step):
        other = (y + step) % NY
        return other, {"inner": 4 * other + 2 * xh + c}

    def at_z(step):
        other = (zs + step) % NZ
        return other, {"outer": z0 + other}

    at_core = {"inner": 4 * y + 2 * xh + 1 - c}
    at_swap = {"head": 1 - xl}
    at_half = {"inner": 4 * y + 2 * (1 - xh) + c}

    def remote(src, dst, send_sem, recv_sem, device):
        return pltpu.make_async_remote_copy(
            src_ref=src, dst_ref=dst, send_sem=send_sem, recv_sem=recv_sem,
            device_id=device, device_id_type=pl.DeviceIdType.MESH,
        )

    barrier = pltpu.get_barrier_semaphore()
    x_partners = [(0, xh), (0, 1 - xh), (1, 1 - xh)]
    partners = [at_x(*place) for place in x_partners]
    partners += [at(step)[1] for at in (at_y, at_z) for step in (1, 2, 3)] + [at_core]
    partners += [{**at_z(step)[1], **at_swap} for step in (1, 2, 3)]
    for device in partners:
        pl.semaphore_signal(barrier, inc=1, device_id=device, device_id_type=pl.DeviceIdType.MESH)

    loads = [
        pltpu.make_async_copy(src, dst, in_sem.at[place])
        for place, (src, dst) in enumerate(
            [(k_in, k_buf), (v_in, v_buf), (q_in, q_buf), (g_in, g_buf)]
        )
    ]
    for load in loads:
        load.start()
    mine = pl.ds(pl.multiple_of(xl * DH, DH), DH)
    theirs = pl.ds(pl.multiple_of((1 - xl) * DH, DH), DH)
    loads[0].wait()
    kv_stage[0] = k_buf[:, theirs]
    kv_all[y, c, zs, xl, 0] = k_buf[:, mine]
    loads[1].wait()
    kv_stage[1] = v_buf[:, theirs]
    kv_all[y, c, zs, xl, 1] = v_buf[:, mine]
    pl.semaphore_wait(barrier, len(partners))

    sends = []

    def begin(copy):
        copy.start()
        sends.append(copy)

    def piece_copy(src, zpos, part, send_sem, device):
        return remote(src, kv_all.at[y, c, zpos, part], send_sem, piece_recv.at[zpos, part], device)

    swap = piece_copy(kv_stage, zs, xl, z_send.at[0, 0], at_swap)
    swap.start()
    for step in (1, 3, 2):
        begin(piece_copy(kv_all.at[y, c, zs, xl], zs, xl, z_send.at[step, 0], at_z(step)[1]))

    def query_copy(place):
        pair, other = x_partners[place]
        return remote(
            qg_stage.at[(xl + 1 - pair) % 2], qg_all.at[:, pair, xh], qg_send.at[place],
            qg_recv.at[pair, xh], at_x(pair, other),
        )

    def wait_queries(place):
        pair, other = x_partners[place]
        remote(
            qg_stage.at[0], qg_all.at[:, pair, other], qg_send.at[place], qg_recv.at[pair, other],
            at_x(pair, other),
        ).wait_recv()

    loads[2].wait()
    loads[3].wait()
    for head in range(HQ):
        columns = pl.ds(head * DH, DH)
        qg_stage[head // GROUP, 0, head % GROUP] = q_buf[:, columns]
        qg_stage[head // GROUP, 1, head % GROUP] = g_buf[:, columns]
    begin(query_copy(0))
    begin(query_copy(1))
    qg_all[:, 1, xh] = qg_stage[xl]

    def chunk_copy(ypos, zpos, send_sem, device):
        place = kv_all.at[ypos, c, zpos]
        return remote(place, place, send_sem, chunk_recv.at[ypos, zpos], device)

    def block_copy(ypos, core):
        place = kv_all.at[ypos, core]
        return remote(place, place, c_send.at[ypos], c_recv.at[ypos, core], at_core)

    def forward_copy(step):
        ystep, target = (1, 3) if step % 2 == 0 else (3, 1)
        return chunk_copy(
            (y + ystep) % NY, (zs + step) % NZ, f_send.at[step], at_y(target)[1]
        )

    piece_copy(kv_stage, zs, 1 - xl, z_send.at[0, 0], at_swap).wait_recv()
    for step in (1, 3, 2):
        place = kv_all.at[y, c, zs, 1 - xl]
        begin(piece_copy(place, zs, 1 - xl, z_send.at[step, 1], at_z(step)[1]))
    for step in (0, 1, 3, 2):
        zpos, device = at_z(step)
        if step:
            for part in (xl, 1 - xl):
                piece_copy(kv_stage, zpos, part, z_send.at[0, 0], device).wait_recv()
        for place, ystep in enumerate((1, 3)):
            begin(chunk_copy(y, zpos, y_send.at[place, step], at_y(ystep)[1]))
        if step == 0:
            begin(query_copy(2))
    begin(block_copy(y, c))

    def wait_chunk(ystep, step):
        ypos, device = at_y(ystep)
        chunk_copy(ypos, (zs + step) % NZ, y_send.at[0, 0], device).wait_recv()

    for step in (0, 1, 3, 2):
        for ystep in (1, 3):
            wait_chunk(ystep, step)
            if (step % 2 == 0) == (ystep == 1):
                begin(forward_copy(step))
    for ystep in (1, 3):
        begin(block_copy((y + ystep) % NY, c))
    for place in range(3):
        wait_queries(place)

    queries = qg_all.at[0].reshape(QROWS, DH)
    out_grads = qg_all.at[1].reshape(QROWS, DH)

    stats = [(m_ref, m_other), (l_ref, l_other), (d_ref, d_other)]

    def stat_copy(kind):
        own, other = stats[kind]
        return remote(own, other, stat_send.at[kind], stat_recv.at[kind], at_half)

    def wait_core(ystep):
        block_copy((y + ystep) % NY, 1 - c).wait_recv()

    m_ref[...] = jnp.full_like(m_ref, -1e30)
    l_ref[...] = jnp.zeros_like(l_ref)
    d_ref[...] = jnp.zeros_like(d_ref)

    def stats_step(turn, carry):
        @pl.when(turn == 1)
        def second():
            wait_core(1)

        @pl.when(turn == 2)
        def third():
            for step in range(NZ):
                wait_chunk(2, step)
            block_copy((y + 2) % NY, c).start()
            wait_core(3)

        @pl.when(turn == 3)
        def last():
            wait_core(2)

        ypos = (y + turn + turn // 2 - 2 * (turn // 3)) % NY
        keys = kv_all[ypos, :, :, :, 0].reshape(BLOCK, DH)
        values = kv_all[ypos, :, :, :, 1].reshape(BLOCK, DH)
        scores = dot(keys, queries[...], 1, 1)
        prob_grad = dot(values, out_grads[...], 1, 1)
        old = m_ref[...]
        new = jnp.maximum(old, jnp.max(scores, axis=0, keepdims=True) * SCALE2)
        factor = jnp.exp2(old - new)
        weights = jnp.exp2(scores * SCALE2 - new)
        e_ref[ypos] = weights.astype(BF16).reshape(2, BLOCK // 2, QROWS)
        mb_ref[ypos] = new
        m_ref[...] = new
        l_ref[...] = l_ref[...] * factor + jnp.sum(weights, axis=0, keepdims=True)
        d_ref[...] = d_ref[...] * factor + jnp.sum(weights * prob_grad, axis=0, keepdims=True)
        return carry

    wait_core(0)
    lax.fori_loop(0, NY, stats_step, 0)

    for kind in range(3):
        stat_copy(kind).start()
    dq_acc[...] = jnp.zeros_like(dq_acc)
    for kind in range(3):
        stat_copy(kind).wait_recv()
    top = jnp.maximum(m_ref[...], m_other[...])
    own_factor = jnp.exp2(m_ref[...] - top)
    other_factor = jnp.exp2(m_other[...] - top)
    total = l_ref[...] * own_factor + l_other[...] * other_factor
    weighted = d_ref[...] * own_factor + d_other[...] * other_factor
    lse_ref[...] = top + jnp.log2(total)
    mean_ref[...] = weighted / total

    def grad_block(ypos, half):
        keys = kv_all[ypos, :, pl.ds(2 * half, 2), :, 0].reshape(2 * HALF, DH)
        values = kv_all[ypos, :, pl.ds(2 * half, 2), :, 1].reshape(2 * HALF, DH)
        prob_grad = dot(values, out_grads[...], 1, 1)
        place = pl.ds(pl.multiple_of(half * HALF, HALF), HALF)
        factor = jnp.exp2(mb_ref[ypos] - lse_ref[...])
        probs = e_ref[ypos, :, place, :].reshape(2 * HALF, QROWS).astype(F32) * factor
        grad_low = (probs * (prob_grad - mean_ref[...])).astype(BF16)
        value_term = dot(probs.astype(BF16), out_grads[...], 1, 0)
        key_term = dot(grad_low, queries[...], 1, 0) * SCALE
        dq_acc[...] += dot(keys, grad_low, 0, 0)
        shape = (2, 2, 2, ROWS, DH)
        return key_term.reshape(shape), value_term.reshape(shape)

    def core_copy(ypos, half):
        place = pl.ds(2 * half, 2)
        return remote(
            dkv.at[ypos, place], core_rx.at[ypos, place], dc_send.at[ypos, half],
            dc_recv.at[ypos, half], at_core,
        )

    def y_copy(ypos, sender, half, device):
        place = pl.ds(2 * half, 2)
        return remote(
            y_sum.at[ypos, place], y_rx.at[sender, place], dy_send.at[ypos, half],
            dy_recv.at[sender, half], device,
        )

    def y_total(half):
        place = pl.ds(2 * half, 2)
        for step in (1, 2, 3):
            ypos, device = at_y(step)
            y_copy(ypos, ypos, half, device).wait_recv()
        total = y_sum[y, place].astype(F32)
        for step in (1, 2, 3):
            total = total + y_rx[(y + step) % NY, place].astype(F32)
        z_sum[place] = total.astype(BF16)

    def z_copy(zpos, part, place):
        return remote(
            z_sum.at[zpos, part], z_rx.at[zs, xl], dz_send.at[place], dz_recv.at[zs, xl],
            {"outer": z0 + zpos, "head": part},
        )

    def wait_z(zpos, part):
        remote(
            z_sum.at[zpos, part], z_rx.at[zpos, part], dz_send.at[0], dz_recv.at[zpos, part],
            {"outer": z0 + zpos, "head": part},
        ).wait_recv()

    far_places = [(2 * (1 - zq) + place // 2, place % 2, place) for place in range(4)]
    near = 4 * zq + 1 - zs
    near_places = [(near, 0, 4), (near, 1, 5), (zs, 1 - xl, 6)]

    def grad_place(turn):
        late, slot = turn % 2, turn // 2
        half = (1 - late) * (1 - zq) + late * zq
        ystep = ((1 - slot // 2) * (2 - slot) + slot // 2 * (slot + 1)) % NY
        return half, slot, at_y(ystep)

    def put_other(turn):
        half, slot, (ypos, device) = grad_place(turn)
        for kind in range(2):
            dkv[ypos, pl.ds(2 * half, 2), :, kind] = terms[turn % 2, kind, 1 - c].astype(BF16)
        core_copy(ypos, half).start()

    def put_own(turn):
        half, slot, (ypos, device) = grad_place(turn)
        place = pl.ds(2 * half, 2)
        core_copy(ypos, half).wait_recv()
        for kind in range(2):
            total = terms[turn % 2, kind, c] + core_rx[ypos, place, :, kind].astype(F32)
            y_sum[ypos, place, :, kind] = total.astype(BF16)

        @pl.when(slot < NY - 1)
        def send():
            y_copy(ypos, y, half, device).start()

    def grad_step(turn, carry):
        half, slot, (ypos, device) = grad_place(turn)
        for kind, term in enumerate(grad_block(ypos, half)):
            terms[turn % 2, kind] = term
        put_other(turn)

        @pl.when(turn > 0)
        def last_turn():
            put_own(turn - 1)

        return carry

    lax.fori_loop(0, 2 * NY, grad_step, 0)
    for pair in (1, 0):
        done = (dq_acc[:, pl.ds(pair * PAIR, PAIR)] * SCALE).T.astype(BF16)
        dq_stage[pair] = done.reshape(2, GROUP, ROWS, DH)
        for place, (of_pair, other) in enumerate(x_partners):
            if of_pair == pair:
                begin(
                    remote(
                        dq_stage.at[pair, other], dq_rx.at[pair, xh], dq_send.at[place],
                        dq_recv.at[pair, xh], at_x(pair, other),
                    )
                )
    y_total(1 - zq)
    for far in far_places:
        z_copy(*far).start()
    dq_rx[1, xh] = dq_stage[1, xh]
    put_own(2 * NY - 1)
    y_total(zq)
    for near_place in near_places:
        z_copy(*near_place).start()
    z_rx[zs, xl] = z_sum[zs, xl]
    for step in (2, 3, 1):
        for part in range(2):
            wait_z(at_z(step)[0], part)
    wait_z(zs, 1 - xl)
    for head in range(HK):
        total = z_rx[0, head].astype(F32)
        for zpos in range(1, NZ):
            total = total + z_rx[zpos, head].astype(F32)
        dk_out[:, pl.ds(head * DH, DH)] = total[0].astype(BF16)
        dv_out[:, pl.ds(head * DH, DH)] = total[1].astype(BF16)

    for pair, other in x_partners:
        remote(
            dq_stage.at[0, 0], dq_rx.at[pair, other], dq_send.at[0], dq_recv.at[pair, other],
            at_x(pair, other),
        ).wait_recv()
    for head in range(HQ):
        group, place = head // GROUP, head % GROUP
        pair = (xl + group + 1) % 2
        both = dq_rx[pair, 0, place].astype(F32) + dq_rx[pair, 1, place].astype(F32)
        dq_out[:, pl.ds(head * DH, DH)] = both.astype(BF16)

    for copy in sends:
        copy.wait_send()
    swap.wait_send()
    for kind in range(3):
        stat_copy(kind).wait_send()
    block_copy((y + 2) % NY, c).wait_send()
    for place in far_places + near_places:
        z_copy(*place).wait_send()
    for half in range(2):
        for ypos in range(NY):
            core_copy(ypos, half).wait_send()
        for step in (1, 2, 3):
            ypos, device = at_y(step)
            y_copy(ypos, y, half, device).wait_send()


def on_device(query, key, value, grad_out):
    vmem = pl.BlockSpec(memory_space=pltpu.VMEM)
    dma = pltpu.SemaphoreType.DMA
    rows = query.shape[0]
    return pl.pallas_call(
        kernel,
        out_shape=(
            pltpu.VMEM(query.shape, BF16),
            pltpu.VMEM(key.shape, BF16),
            pltpu.VMEM(value.shape, BF16),
        ),
        in_specs=[pl.BlockSpec(memory_space=pl.ANY)] * 4,
        out_specs=(vmem,) * 3,
        scratch_shapes=[
            pltpu.VMEM((rows, HQ * DH), BF16),
            pltpu.VMEM((rows, HK * DH), BF16),
            pltpu.VMEM((rows, HK * DH), BF16),
            pltpu.VMEM((rows, HQ * DH), BF16),
            pltpu.VMEM((HK, 2, GROUP, ROWS, DH), BF16),
            pltpu.VMEM((2, ROWS, DH), BF16),
            pltpu.VMEM((2, 2, 2, GROUP, ROWS, DH), BF16),
            pltpu.VMEM((NY, 2, NZ, 2, 2, ROWS, DH), BF16),
            pltpu.VMEM((NY, 2, BLOCK // 2, QROWS), BF16),
            pltpu.VMEM((NY, 1, QROWS), F32),
            pltpu.VMEM((1, QROWS), F32),
            pltpu.VMEM((1, QROWS), F32),
            pltpu.VMEM((1, QROWS), F32),
            pltpu.VMEM((1, QROWS), F32),
            pltpu.VMEM((1, QROWS), F32),
            pltpu.VMEM((1, QROWS), F32),
            pltpu.VMEM((1, QROWS), F32),
            pltpu.VMEM((1, QROWS), F32),
            pltpu.VMEM((DH, QROWS), F32),
            pltpu.VMEM((2, 2, 2, 2, 2, ROWS, DH), F32),
            pltpu.VMEM((NY, NZ, 2, 2, ROWS, DH), BF16),
            pltpu.VMEM((NY, NZ, 2, 2, ROWS, DH), BF16),
            pltpu.VMEM((NY, NZ, 2, 2, ROWS, DH), BF16),
            pltpu.VMEM((NY, NZ, 2, 2, ROWS, DH), BF16),
            pltpu.VMEM((NZ, 2, 2, ROWS, DH), BF16),
            pltpu.VMEM((NZ, 2, 2, ROWS, DH), BF16),
            pltpu.VMEM((2, 2, GROUP, ROWS, DH), BF16),
            pltpu.VMEM((2, 2, GROUP, ROWS, DH), BF16),
            dma((4,)),
            dma((3,)),
            dma((2, 2)),
            dma((NZ, 2)),
            dma((NZ, 2)),
            dma((2, NZ)),
            dma((NZ,)),
            dma((NY, NZ)),
            dma((NY,)),
            dma((NY, 2)),
            dma((3,)),
            dma((3,)),
            dma((NY, 2)),
            dma((NY, 2)),
            dma((NY, 2)),
            dma((NY, 2)),
            dma((7,)),
            dma((NZ, 2)),
            dma((3,)),
            dma((2, 2)),
        ],
        compiler_params=pltpu.CompilerParams(
            collective_id=0, has_side_effects=True, vmem_limit_bytes=60 * 2**20
        ),
    )(query, key, value, grad_out)

def solution(mesh):
    spec = P(("head", "inner", "outer"), None)
    return jax.shard_map(
        on_device, mesh=mesh, in_specs=(spec,) * 4, out_specs=(spec,) * 3, check_vma=False
    )
```
